32 devices in a mesh: gx: 4 (over z), gy: 4 (over y, x), gz: 2 (over core).
Axes of the slice: x: 2, y: 2, z: 4, core: 2. Of those that a mesh axis runs over, the one named last changes fastest.
Arguments:
- points: float32 [1024, 3, 128], P(('gx', 'gy', 'gz')), may hold values from -6 to 6
- source: float32 [1024, 128], P(('gx', 'gy', 'gz')), may hold values from -6 to 6
- density: float32 [1024, 128], P(('gx', 'gy', 'gz')), may hold values from -3 to 3
- anterp: bfloat16 [1024, 216, 128], P(('gx', 'gy', 'gz')), may hold values from -0.5 to 0.5
- child_slot: int32 [1024], P(('gx', 'gy', 'gz')), may hold values from 0 to 7, as said below
- child_ops: bfloat16 [8, 216, 216], replicated, may hold values from -0.4375 to 0.4375
- parent: int32 [1024], P(('gx', 'gy', 'gz')), may hold values from 0 to 127, as said below
- near_list: int32 [1024, 27], P(('gx', 'gy', 'gz')), may hold values from -1 to 1023, as said below
- far_list: int32 [128, 189], P(('gx', 'gy', 'gz')), may hold values from 0 to 127
- far_op: int32 [128, 189], P(('gx', 'gy', 'gz')), may hold values from 0 to 15
- translations: bfloat16 [16, 216, 216], replicated, may hold values from -0.03125 to 0.03125
Outputs:
- density_out: float32 [1024, 128], P(('gx', 'gy', 'gz'))
- potential: float32 [1024, 128], P(('gx', 'gy', 'gz'))
The draws below stay inside these ranges and needn't reach their ends.
Inputs may be any that keep to these rules, and one draw needn't show every extreme that they name: Every octant has exactly 8 child leaves. Leaf l of device d = l // 32 has a parent octant owned by d or by a device next to d along gz with the same gx and gy index: parent // 4 is d - 1, d or d + 1, never past the ends of gz. `child_slot`: the 8 children of one octant have 8 different positions. `near_list`: row l lists distinct leaves: entry 0 is l itself, then other leaves b with |b - l| <= 13 on devices with the same gx and gy index as l's, then -1 in the remaining slots; at least 9 entries are listed.
All inputs are finite; a program needn't handle non-finite values.
Results may differ from the reference program's by a relative error of at most 0.008.
Values may be sent and summed in bfloat16 or wider, within the bound.
No kernel may reach another device: no remote copies, remote signals or barrier semaphores. Data moves between devices by JAX's collectives and lax.ppermute only.
A program may use at most 64 MiB of HBM per device.

```python
import jax
import jax.numpy as jnp
from jax import lax

PTS = 128
NODES = 216
OPS = 16
INTER = 189
GHOST = 13
ITERS = 2
LEAF_DEV = 32
OCT_DEV = 4
NEAR = 27
LEAVES = 1024
OCTS = 128
N_GZ = 2


def tree_layout(key):
    base = jax.random.fold_in(key, 11)
    key_cut, key_perm = jax.random.split(base)
    leaf_ids = jnp.arange(LEAVES, dtype=jnp.int32)
    device = leaf_ids // LEAF_DEV
    within = leaf_ids % LEAF_DEV
    column = device % N_GZ
    cuts = jax.random.randint(key_cut, (LEAVES // LEAF_DEV,), 1, 4).astype(jnp.int32)
    cut_after = jnp.take(cuts, device, axis=0)
    cut_before = jnp.take(cuts, jnp.maximum(device - 1, 0), axis=0)
    to_upper = (column < N_GZ - 1) & (within >= LEAF_DEV - cut_after)
    to_lower = (column > 0) & (within < cut_before)
    parent = jnp.where(to_upper, (device + 1) * OCT_DEV, jnp.where(to_lower, device * OCT_DEV - 1, device * OCT_DEV + within // 8))
    position = jnp.where(to_upper, within - (LEAF_DEV - cut_after), jnp.where(to_lower, 8 - cut_before + within, within % 8))
    scores = jax.random.randint(key_perm, (OCTS, 8), 0, 1 << 20) * 8 + jnp.arange(8, dtype=jnp.int32)[None, :]
    perms = jnp.argsort(scores, axis=1).astype(jnp.int32)
    slots = perms[parent, position]
    return (parent.astype(jnp.int32), slots.astype(jnp.int32))


def draw_parent(key, part):
    return tree_layout(key)[0]


def draw_child_slot(key, part):
    return tree_layout(key)[1]


def draw_near_list(key, part):
    leaf_ids = jnp.arange(LEAVES, dtype=jnp.int32)
    others = jnp.concatenate([jnp.arange(-GHOST, 0, dtype=jnp.int32), jnp.arange(1, GHOST + 1, dtype=jnp.int32)])
    key_order, key_count = jax.random.split(jax.random.fold_in(key, 23))
    ranks = jax.random.randint(key_order, (LEAVES, 2 * GHOST), 0, 1 << 20) * (2 * GHOST) + jnp.arange(2 * GHOST, dtype=jnp.int32)[None, :]
    targets = leaf_ids[:, None] + others[None, :]
    group_here = leaf_ids // LEAF_DEV // N_GZ
    same_group = (targets >= 0) & (targets < LEAVES) & (jnp.maximum(targets, 0) // LEAF_DEV // N_GZ == group_here[:, None])
    scores = jnp.where(same_group, ranks, ranks + (1 << 27))
    order = jnp.argsort(scores, axis=1)
    ordered = jnp.take_along_axis(targets, order, axis=1)
    counts = jax.random.randint(key_count, (LEAVES,), 9, NEAR + 1)
    counts = jnp.where(leaf_ids == 0, 9, counts)
    counts = jnp.minimum(counts, 1 + jnp.sum(same_group.astype(jnp.int32), axis=1))
    full_list = jnp.concatenate([leaf_ids[:, None], ordered], axis=1)
    positions = jnp.arange(NEAR, dtype=jnp.int32)
    return jnp.where(positions[None, :] < counts[:, None], full_list, -1).astype(jnp.int32)


def place_ends(values, rng, low, largest):
    longest = values.shape.index(max(values.shape))
    spots = []
    for shift in (0, 1):
        where = [jax.random.randint(jax.random.fold_in(rng, axis), (), 0, length) for axis, length in enumerate(values.shape)]
        where[longest] = (where[longest] + shift) % values.shape[longest]
        spots.append(tuple(where))
    return values.at[spots[0]].set(low).at[spots[1]].set(largest)


def shard_levels(stream_key, shape, pieces, least, top_value):
    def one(dim, parts):
        heights = jax.random.uniform(jax.random.fold_in(jax.random.fold_in(stream_key, 6), dim), (parts,), jnp.float32, least / len(pieces), top_value / len(pieces))
        return jnp.repeat(jnp.exp(heights), shape[dim] // parts).reshape((-1,) + (1,) * (len(shape) - dim - 1))

    loudness = one(*pieces[0])
    for cut in pieces[1:]:
        loudness = loudness * one(*cut)
    return loudness


def normal_values(key, extent, width, bound, cuts=(), kind=jnp.bfloat16):
    entries = width * jax.random.normal(key, extent, jnp.float32)
    if cuts:
        entries = entries * shard_levels(key, extent, cuts, -0.22, 0.18)
    return jnp.clip(entries, -bound, bound).astype(kind)


def setup_inputs(seed: int = 0) -> dict:
    arg_keys = jax.random.split(jax.random.key(seed), 12)
    return {
        "points": normal_values(arg_keys[0], (LEAVES, 3, PTS), 1.0, 6.0, ((0, 32),), jnp.float32),
        "source": normal_values(arg_keys[1], (LEAVES, PTS), 1.0, 6.0, ((0, 32),), jnp.float32),
        "density": normal_values(arg_keys[2], (LEAVES, PTS), 0.5, 3.0, ((0, 32),), jnp.float32),
        "anterp": normal_values(arg_keys[3], (LEAVES, NODES, PTS), PTS ** -0.5, 0.5, ((0, 32),)),
        "child_slot": draw_child_slot(jax.random.fold_in(arg_keys[11], 71), 0),
        "child_ops": normal_values(arg_keys[5], (8, NODES, NODES), NODES ** -0.5, 0.4375),
        "parent": draw_parent(jax.random.fold_in(arg_keys[11], 71), 0),
        "near_list": draw_near_list(jax.random.fold_in(arg_keys[11], 71), 0),
        "far_list": place_ends(jax.random.randint(arg_keys[8], (OCTS, INTER), 0, OCTS), jax.random.fold_in(arg_keys[8], 1), 0, OCTS - 1).astype(jnp.int32),
        "far_op": place_ends(jax.random.randint(arg_keys[9], (OCTS, INTER), 0, OPS), jax.random.fold_in(arg_keys[9], 1), 0, OPS - 1).astype(jnp.int32),
        "translations": normal_values(arg_keys[10], (OPS, NODES, NODES), (NODES * INTER) ** -0.5, 0.03125),
    }


SOFTEN = 0.01
DAMPING = 0.5
FAR_WEIGHT = 0.3
NEAR_WEIGHT = 0.03

def kernel_sum(target, near_points, weights):
    squared = jnp.zeros((near_points.shape[0], target.shape[1], near_points.shape[2]), jnp.float32)
    for component in range(3):
        comp_gap = target[component][None, :, None] - near_points[:, component][:, None, :]
        squared = squared + comp_gap * comp_gap
    kernel_tile = 1.0 / jnp.sqrt(squared + SOFTEN)
    return lax.optimization_barrier(jnp.sum(kernel_tile * weights[:, None, :], axis=(0, 2)))

def select_child(by_child, child_slot):
    positions = jnp.arange(8, dtype=jnp.int32)
    return lax.optimization_barrier(jnp.sum(jnp.where(child_slot[:, None, None] == positions[None, :, None], by_child, 0.0), axis=1))

def reference(points, source, density, anterp, child_slot, child_ops, parent, near_list, far_list, far_op, translations):
    highest = lax.Precision.HIGHEST
    anterp_wide = anterp.astype(jnp.float32)
    child_wide = child_ops.astype(jnp.float32)
    trans_wide = translations.astype(jnp.float32)
    op_ids = jnp.arange(OPS, dtype=jnp.int32)
    density_now = density
    potential = density
    for step in range(ITERS):

        def one_leaf(leaf_id):
            listed = near_list[leaf_id]
            is_valid = listed >= 0
            safe_ids = jnp.where(is_valid, listed, 0).astype(jnp.int32)
            near_points = jnp.take(points, safe_ids, axis=0)
            weights = jnp.where(is_valid[:, None], jnp.take(density_now, safe_ids, axis=0), 0.0)
            return kernel_sum(points[leaf_id], near_points, weights)
        near_field = lax.map(one_leaf, jnp.arange(points.shape[0], dtype=jnp.int32))
        density_b = density_now.astype(jnp.bfloat16).astype(jnp.float32)
        leaf_mult = jnp.einsum('lnp,lp->ln', anterp_wide, density_b, precision=highest).astype(jnp.bfloat16)
        by_child = jnp.einsum('cnm,lm->lcn', child_wide, leaf_mult.astype(jnp.float32), precision=highest)
        contrib = select_child(by_child, child_slot)
        multipole = jax.ops.segment_sum(contrib, parent, num_segments=OCTS).astype(jnp.bfloat16)
        multi_wide = multipole.astype(jnp.float32)

        def one_octant(octant_rows):
            listed, chosen = octant_rows
            sources = jnp.take(multi_wide, listed, axis=0)
            picked = (chosen[:, None] == op_ids[None, :]).astype(jnp.float32)
            grouped = jnp.dot(picked.T, sources, precision=highest)
            return jnp.einsum('onm,om->n', trans_wide, grouped, precision=highest)
        local_exp = lax.map(one_octant, (far_list, far_op)).astype(jnp.bfloat16)
        parent_local = jnp.take(local_exp, parent, axis=0).astype(jnp.float32)
        back_child = jnp.einsum('cnm,ln->lcm', child_wide, parent_local, precision=highest)
        leaf_local = select_child(back_child, child_slot).astype(jnp.bfloat16)
        far_field = jnp.einsum('lnp,ln->lp', anterp_wide, leaf_local.astype(jnp.float32), precision=highest)
        potential = FAR_WEIGHT * far_field + NEAR_WEIGHT * near_field
        density_now = density_now + DAMPING * (jnp.tanh(source - potential) - density_now)
    return (density_now, potential)
```

```python
import functools

import jax
import jax.numpy as jnp
from jax import lax
from jax.experimental import pallas as pl
from jax.experimental.pallas import tpu as pltpu
from jax.sharding import PartitionSpec as P

AXES = ("gx", "gy", "gz")
GHOST = 13
ITERS = 2
CHILDREN = 8

SOFTEN = 0.01
DAMPING = 0.5
FAR_WEIGHT = 0.3
NEAR_WEIGHT = 0.03

BF16 = jnp.bfloat16
F32 = jnp.float32
NT = (((1,), (1,)), ((), ()))
VMEM = pl.BlockSpec(memory_space=pltpu.VMEM)
SMEM = pl.BlockSpec(memory_space=pltpu.SMEM)


def dot(a, b):
    return jnp.dot(a, b, preferred_element_type=F32)


def dot_nt(a, b):
    return lax.dot_general(a, b, NT, preferred_element_type=F32)


def three_parts(x):
    high = x.astype(BF16).astype(F32)
    rest = x - high
    middle = rest.astype(BF16).astype(F32)
    return high, middle, rest - middle


def features(leaf_points):
    width = leaf_points.shape[1]
    x = jnp.concatenate([leaf_points, jnp.zeros((5, width), F32)], 0)
    row = lax.broadcasted_iota(jnp.int32, x.shape, 0)
    high, middle, low = three_parts(x)
    norm = jnp.broadcast_to(jnp.sum(x * x, axis=0, keepdims=True), x.shape)
    nh, nm, nl = three_parts(norm)
    eh, em, el = three_parts(norm + SOFTEN)
    zero = jnp.zeros_like(x)
    last = jnp.where(row < 6, 1.0, 0.0)
    source_norm = jnp.where(row == 0, nh, jnp.where(row == 1, nm, jnp.where(row == 2, nl, last)))
    first = jnp.where(row < 3, 1.0, 0.0)
    target_norm = jnp.where(row == 3, eh, jnp.where(row == 4, em, jnp.where(row == 5, el, first)))
    source = [high, high, middle, middle, high, low, source_norm, zero]
    target = [-2 * high, -2 * middle, -2 * high, -2 * middle, -2 * low, -2 * high, target_norm, zero]
    return jnp.concatenate(source, 0), jnp.concatenate(target, 0)


def near_kernel(slots_ref, points_ref, q_ref, out_ref, source_s, target_s, acc_s):
    leaves, near = slots_ref.shape
    width = out_ref.shape[1]

    def build(b, carry):
        source_s[b] = features(points_ref[b])[0].astype(BF16)
        return carry

    lax.fori_loop(0, points_ref.shape[0], build, 0, unroll=4)

    def build_target(b, carry):
        target_s[b] = features(points_ref[b])[1].T.astype(BF16)
        return carry

    lax.fori_loop(0, leaves, build_target, 0, unroll=4)

    def target(leaf, carry):
        rows = target_s[leaf]
        acc = jnp.zeros((width, width), F32)
        for k in range(0, near, 2):
            sources, weights = [], []
            for slot in (k, k + 1):
                if slot < near:
                    index = slots_ref[leaf, slot]
                    scale = jnp.where(index >= 0, 1.0, 0.0)
                    index = jnp.maximum(index, 0)
                    sources.append(source_s[index])
                    weights.append(q_ref[pl.ds(index, 1)] * scale)
            tile = lax.rsqrt(dot(rows, jnp.concatenate(sources, 1)))
            tile = tile * jnp.concatenate(weights, 1)
            for part in range(len(sources)):
                acc = acc + tile[:, part * width : (part + 1) * width]
        acc_s[leaf] = acc
        return carry

    lax.fori_loop(0, leaves, target, 0, unroll=2)

    def finish(leaf, carry):
        out_ref[pl.ds(leaf, 1), :] = jnp.sum(acc_s[leaf].T, axis=0, keepdims=True)
        return carry

    lax.fori_loop(0, leaves, finish, 0, unroll=4)


def near_field(slots, points_ext, q_ext):
    leaves, near = slots.shape
    sources, _, width = points_ext.shape
    pairs = leaves * near * width * width
    return pl.pallas_call(
        near_kernel,
        out_shape=jax.ShapeDtypeStruct((leaves, width), F32),
        in_specs=[SMEM, VMEM, VMEM],
        out_specs=VMEM,
        scratch_shapes=[
            pltpu.VMEM((sources, 64, width), BF16),
            pltpu.VMEM((leaves, width, 64), BF16),
            pltpu.VMEM((leaves, width, width), F32),
        ],
        compiler_params=pltpu.CompilerParams(vmem_limit_bytes=24 << 20),
        cost_estimate=pl.CostEstimate(flops=pairs * 128, bytes_accessed=1 << 20, transcendentals=pairs),
        name="near_field",
    )(slots, points_ext, q_ext)


def child_rows(code, rows):
    index = lax.broadcasted_iota(jnp.int32, (rows, code.shape[1]), 0)
    return jnp.where(index == code, 1.0, 0.0).astype(BF16)


def upward(density, code, anterp_ref, child_ref, table_ref, mult_s):
    leaves = anterp_ref.shape[0]
    slots = table_ref.shape[1]
    density_b = density.astype(BF16)
    for leaf in range(leaves):
        mult_s[leaf : leaf + 1, :] = dot_nt(density_b[leaf : leaf + 1], anterp_ref[leaf])
    by_child = dot(child_rows(code, CHILDREN * slots), mult_s[...].astype(BF16)).astype(BF16)
    part = jnp.zeros((slots, mult_s.shape[1]), F32)
    for child in range(CHILDREN):
        part = part + dot_nt(by_child[child * slots : (child + 1) * slots], child_ref[child])
    part = part.astype(BF16)
    for device in range(table_ref.shape[0]):
        table_ref[device] = part


def downward(tables_ref, counts_ref, trans_ref, code, anterp_ref, child_ref, far_s):
    devices, slots, nodes = tables_ref.shape
    leaves = anterp_ref.shape[0]
    tables = tables_ref[...].reshape(devices * slots, nodes)
    grouped = dot(counts_ref[...], tables).astype(BF16)
    local = jnp.zeros((slots, nodes), F32)
    for op in range(trans_ref.shape[0]):
        local = local + dot_nt(grouped[op * slots : (op + 1) * slots], trans_ref[op])
    local = local.astype(BF16)
    back = [dot(local, child_ref[child]) for child in range(CHILDREN)]
    back = jnp.concatenate(back, 0).astype(BF16)
    pick = child_rows(code, CHILDREN * slots)
    leaf_local = lax.dot_general(pick, back, (((0,), (0,)), ((), ())), preferred_element_type=F32)
    leaf_local = leaf_local.astype(BF16)
    for leaf in range(leaves):
        far_s[leaf : leaf + 1, :] = dot(leaf_local[leaf : leaf + 1], anterp_ref[leaf])
    return far_s[...]


def update(density, source, far, near):
    potential = FAR_WEIGHT * far + NEAR_WEIGHT * near
    return density + DAMPING * (jnp.tanh(source - potential) - density), potential


def first_kernel(q_ref, code_ref, anterp_ref, child_ref, table_ref, mult_s):
    upward(q_ref[...], code_ref[...], anterp_ref, child_ref, table_ref, mult_s)


def middle_kernel(
    tables_ref, counts_ref, trans_ref, near_ref, source_ref, q_ref, code_ref, anterp_ref, child_ref,
    new_q_ref, table_ref, mult_s, far_s,
):
    code = code_ref[...]
    far = downward(tables_ref, counts_ref, trans_ref, code, anterp_ref, child_ref, far_s)
    new_q, _ = update(q_ref[...], source_ref[...], far, near_ref[...])
    new_q_ref[...] = new_q
    upward(new_q, code, anterp_ref, child_ref, table_ref, mult_s)


def last_kernel(
    tables_ref, counts_ref, trans_ref, near_ref, source_ref, q_ref, code_ref, anterp_ref, child_ref,
    new_q_ref, potential_ref, far_s,
):
    code = code_ref[...]
    far = downward(tables_ref, counts_ref, trans_ref, code, anterp_ref, child_ref, far_s)
    new_q, potential = update(q_ref[...], source_ref[...], far, near_ref[...])
    new_q_ref[...] = new_q
    potential_ref[...] = potential


def counts_kernel(pair, octs, far_list_ref, far_op_ref, counts_ref, rows_s):
    slots, inter = far_list_ref.shape
    rows, columns = counts_ref.shape
    ops = rows // slots
    column = lax.broadcasted_iota(jnp.int32, (columns, inter), 0)
    device, slot = column // slots, column % slots
    octant = (device // 2 * 2 if pair else device - 1) * octs + slot
    op = lax.broadcasted_iota(jnp.int32, (ops, inter), 0)
    for g in range(slots):
        source = jnp.where(octant == far_list_ref[g : g + 1], 1.0, 0.0).astype(BF16)
        chosen = jnp.where(op == far_op_ref[g : g + 1], 1.0, 0.0).astype(BF16)
        rows_s[:, g, :] = dot_nt(chosen, source)
    counts_ref[...] = rows_s[...].reshape(rows, columns).astype(BF16)


def params():
    return pltpu.CompilerParams(vmem_limit_bytes=24 << 20)


def swap(array):
    return lax.ppermute(array, "gz", [(0, 1), (1, 0)])


def extend(array, width):
    count = lax.axis_size("gz")
    if count == 2:
        return jnp.concatenate([array, swap(array)], 0)
    up = [(i, i + 1) for i in range(count - 1)]
    down = [(i + 1, i) for i in range(count - 1)]
    after = lax.ppermute(array[:width], "gz", down)
    before = lax.ppermute(array[-width:], "gz", up)
    return jnp.concatenate([array, after, before], 0)


def octant_window(array):
    count = lax.axis_size("gz")
    if count == 2:
        other = swap(array)
        low = lax.axis_index("gz") == 0
        return jnp.where(low, jnp.concatenate([array, other], 0), jnp.concatenate([other, array], 0))
    up = [(i, i + 1) for i in range(count - 1)]
    down = [(i + 1, i) for i in range(count - 1)]
    rows = [lax.ppermute(array, "gz", up), array, lax.ppermute(array, "gz", down)]
    rows = jnp.concatenate(rows, 0)
    return jnp.pad(rows, ((0, -rows.shape[0] % 8), (0, 0)))


def shards(
    points, source, density, anterp, child_slot, child_ops, parent, near_list, far_list, far_op, translations
):
    leaves, _, width = points.shape
    octs, inter = far_list.shape
    ops, nodes, _ = translations.shape
    devices = lax.axis_size(AXES)
    pair = lax.axis_size("gz") == 2
    device = lax.axis_index(AXES)
    halo = -(-GHOST // 8) * 8

    window = octant_window(far_list * ops + far_op)
    slots = window.shape[0]
    base_oct = (device // 2 * 2 if pair else device - 1) * octs
    code = (child_slot * slots + (parent - base_oct))[None, :]
    points_ext = extend(points, halo)
    near_slots = jnp.where(near_list >= 0, (near_list - device * leaves) % points_ext.shape[0], -1)

    counts = pl.pallas_call(
        functools.partial(counts_kernel, pair, octs),
        out_shape=jax.ShapeDtypeStruct((ops * slots, devices * slots), BF16),
        in_specs=[VMEM, VMEM],
        out_specs=VMEM,
        scratch_shapes=[pltpu.VMEM((ops, slots, devices * slots), F32)],
        compiler_params=params(),
        name="interaction_counts",
    )(window // ops, window % ops)

    table_shape = jax.ShapeDtypeStruct((devices, slots, nodes), BF16)
    field_shape = jax.ShapeDtypeStruct((leaves, width), F32)
    mult_scratch = pltpu.VMEM((leaves, nodes), F32)
    far_scratch = pltpu.VMEM((leaves, width), F32)

    table = pl.pallas_call(
        first_kernel,
        out_shape=table_shape,
        in_specs=[VMEM] * 4,
        out_specs=VMEM,
        scratch_shapes=[mult_scratch],
        compiler_params=params(),
        name="upward_pass",
    )(density, code, anterp, child_ops)

    density_now = density
    for step in range(ITERS):
        tables = lax.all_to_all(table, AXES, 0, 0, tiled=True)
        near = near_field(near_slots, points_ext, extend(density_now, halo))
        operands = (tables, counts, translations, near, source, density_now, code, anterp, child_ops)
        if step < ITERS - 1:
            density_now, table = pl.pallas_call(
                middle_kernel,
                out_shape=(field_shape, table_shape),
                in_specs=[VMEM] * 9,
                out_specs=(VMEM, VMEM),
                scratch_shapes=[mult_scratch, far_scratch],
                compiler_params=params(),
                name="downward_upward",
            )(*operands)
        else:
            density_now, potential = pl.pallas_call(
                last_kernel,
                out_shape=(field_shape, field_shape),
                in_specs=[VMEM] * 9,
                out_specs=(VMEM, VMEM),
                scratch_shapes=[far_scratch],
                compiler_params=params(),
                name="downward_pass",
            )(*operands)
    return density_now, potential


def solution(mesh):
    rows = P(AXES, None)
    blocks = P(AXES, None, None)
    line = P(AXES)
    in_specs = (blocks, rows, rows, blocks, line, P(), line, rows, rows, rows, P())
    return jax.shard_map(shards, mesh=mesh, in_specs=in_specs, out_specs=(rows, rows), check_vma=False)
```

```python
import functools

import jax
import jax.numpy as jnp
from jax import lax
from jax.experimental import pallas as pl
from jax.experimental.pallas import tpu as pltpu
from jax.sharding import PartitionSpec as P

AXES = ("gx", "gy", "gz")
GHOST = 13
ITERS = 2
CHILDREN = 8

SOFTEN = 0.01
DAMPING = 0.5
FAR_WEIGHT = 0.3
NEAR_WEIGHT = 0.03

BF16 = jnp.bfloat16
F32 = jnp.float32
UNROLL = 8
M2L_LOOP = 2
L2L_LOOP = 2
CHUNKS = 2
LATER_MIB = 6
NT = (((1,), (1,)), ((), ()))
VMEM = pl.BlockSpec(memory_space=pltpu.VMEM)
SMEM = pl.BlockSpec(memory_space=pltpu.SMEM)
HBM = pl.BlockSpec(memory_space=pltpu.HBM)


def in_hbm(array):
    return pltpu.with_memory_space_constraint(array, pltpu.HBM)


def dot(a, b):
    return jnp.dot(a, b, preferred_element_type=F32)


def dot_nt(a, b):
    return lax.dot_general(a, b, NT, preferred_element_type=F32)


def three_parts(x):
    high = x.astype(BF16).astype(F32)
    rest = x - high
    middle = rest.astype(BF16).astype(F32)
    return high, middle, rest - middle


def features(x):
    row = lax.broadcasted_iota(jnp.int32, x.shape, 0)
    high, middle, low = three_parts(x)
    norm = jnp.broadcast_to(jnp.sum(x * x, axis=0, keepdims=True), x.shape)
    nh, nm, nl = three_parts(norm)
    eh, em, el = three_parts(norm + SOFTEN)
    zero = jnp.zeros_like(x)
    last = jnp.where(row < 6, 1.0, 0.0)
    source_norm = jnp.where(row == 0, nh, jnp.where(row == 1, nm, jnp.where(row == 2, nl, last)))
    first = jnp.where(row < 3, 1.0, 0.0)
    target_norm = jnp.where(row == 3, eh, jnp.where(row == 4, em, jnp.where(row == 5, el, first)))
    source = [high, high, middle, middle, high, low, source_norm, zero]
    target = [-2 * high, -2 * middle, -2 * high, -2 * middle, -2 * low, -2 * high, target_norm, zero]
    return jnp.concatenate(source, 0), jnp.concatenate(target, 0)


def coordinates(points_ref, leaf):
    x, y, z = [points_ref[c, pl.ds(leaf, 1), :] for c in range(3)]
    row = lax.broadcasted_iota(jnp.int32, (8, x.shape[1]), 0)
    return jnp.where(row == 0, x, jnp.where(row == 1, y, jnp.where(row == 2, z, 0.0)))


def other_row(pair, low, leaf, leaves):
    return jnp.where(low, leaf, leaves - 1 - leaf) if pair else leaf


def near_part(
    pair, first, count, listed_ref, points_ref, points_other_ref, q_ref, q_other_ref, out_ref,
    source_s, target_s, q_s, ahead_s, back_s,
):
    leaves, width = out_ref.shape
    reach = GHOST + 1
    stop = first + count
    end = stop + GHOST
    low = lax.axis_index("gz") == 0 if pair else True

    def place(i):
        return jnp.where(low, i, leaves - 1 - i) if pair else i

    def own(i, carry):
        leaf = place(i)
        source, target = features(coordinates(points_ref, leaf))
        source_s[i] = source.astype(BF16)
        target_s[i] = target.T.astype(BF16)
        q_s[pl.ds(i, 1), :] = q_ref[pl.ds(leaf, 1), :]
        return carry

    def own_source(i, carry):
        leaf = place(i)
        source_s[i] = features(coordinates(points_ref, leaf))[0].astype(BF16)
        q_s[pl.ds(i, 1), :] = q_ref[pl.ds(leaf, 1), :]
        return carry

    def other(i, carry):
        leaf = other_row(pair, low, i, leaves)
        source_s[leaves + i] = features(coordinates(points_other_ref, leaf))[0].astype(BF16)
        q_s[pl.ds(leaves + i, 1), :] = q_other_ref[pl.ds(leaf, 1), :]
        return carry

    lax.fori_loop(first, stop, own, 0, unroll=4)
    lax.fori_loop(stop, min(end, leaves), own_source, 0, unroll=4)
    lax.fori_loop(0, max(end - leaves, 0), other, 0, unroll=4)

    def target(i, carry):
        rows = target_s[i]
        mine = jnp.broadcast_to(q_s[pl.ds(i, 1), :], (width, width)).T
        acc = jnp.zeros((width, width), F32)
        for d in range(0, reach, 2):
            sources = [source_s[i + d], source_s[i + d + 1]]
            tiles = lax.rsqrt(dot(rows, jnp.concatenate(sources, 1)))
            for part in (0, 1):
                shift = d + part
                tile = tiles[:, part * width : (part + 1) * width]
                acc = acc + tile * (q_s[pl.ds(i + shift, 1), :] * listed_ref[place(i), i + shift])
                if shift:
                    inside = i + shift < leaves
                    weight = listed_ref[place(jnp.minimum(i + shift, leaves - 1)), i]
                    weight = jnp.where(inside, weight, 0.0)
                    back = jnp.sum((tile * mine).reshape(width // 8, 8, width), axis=0)
                    back_s[i + shift, shift - 1] = back * weight
        ahead_s[i] = jnp.sum(acc.T.reshape(width // 8, 8, width), axis=0)
        return carry

    lax.fori_loop(first, stop, target, 0, unroll=min(count, UNROLL))

    if not pair and first == 0:
        halo = q_other_ref.shape[0] // 2
        lax.fori_loop(halo, 2 * halo, other, 0)

        def behind(i, carry):
            acc = jnp.zeros((width, width), F32)
            for j in range(leaves + halo, leaves + 2 * halo):
                tile = lax.rsqrt(dot(target_s[i], source_s[j]))
                acc = acc + tile * (q_s[j : j + 1] * listed_ref[i, j])
            ahead_s[i] = ahead_s[i] + jnp.sum(acc.T.reshape(width // 8, 8, width), axis=0)
            return carry

        lax.fori_loop(0, GHOST, behind, 0)

    for i in range(first, min(end, leaves)):
        terms = [ahead_s[i]] if i < stop else []
        terms += [back_s[i, d - 1] for d in range(1, reach) if first <= i - d < stop]
        total = functools.reduce(jnp.add, terms)
        row = pl.ds(place(i), 1)
        out_ref[row, :] = out_ref[row, :] + jnp.sum(total, axis=0, keepdims=True)


def near_scratch(leaves, rows, width):
    return [
        pltpu.VMEM((rows, 64, width), BF16),
        pltpu.VMEM((leaves, width, 64), BF16),
        pltpu.VMEM((rows, width), F32),
        pltpu.VMEM((leaves, 8, width), F32),
        pltpu.VMEM((leaves + GHOST, GHOST, 8, width), F32),
    ]


def near_kernel(
    pair, count, listed_ref, points_ref, points_other_ref, q_ref, q_other_ref, out_ref,
    source_s, target_s, q_s, ahead_s, back_s,
):
    out_ref[...] = jnp.zeros_like(out_ref)
    near_part(
        pair, 0, count, listed_ref, points_ref, points_other_ref, q_ref, q_other_ref, out_ref,
        source_s, target_s, q_s, ahead_s, back_s,
    )


def near_start(pair, count, listed, points, points_other, q, q_other):
    leaves, width = q.shape
    pairs = count * (GHOST + 1) * width * width
    return pl.pallas_call(
        functools.partial(near_kernel, pair, count),
        out_shape=jax.ShapeDtypeStruct((leaves, width), F32),
        in_specs=[SMEM, VMEM, VMEM, VMEM, VMEM],
        out_specs=VMEM,
        scratch_shapes=near_scratch(leaves, listed.shape[1], width),
        compiler_params=params(6),
        cost_estimate=pl.CostEstimate(flops=pairs * 8192, bytes_accessed=1 << 20, transcendentals=pairs),
        name="near_start",
    )(listed, points, points_other, q, q_other)


def leaf_codes(pair, octs, slots, child_slot_ref, parent_ref):
    device = lax.axis_index(AXES)
    first = (device // 2 * 2 if pair else device - 1) * octs
    return child_slot_ref[...] * slots + (parent_ref[...] - first)


def child_rows(code, rows):
    index = lax.broadcasted_iota(jnp.int32, (rows, code.shape[1]), 0)
    return jnp.where(index == code, 1.0, 0.0).astype(BF16)


def leaf_multipoles(by_point, anterp_ref, first, count):
    lane = lax.broadcasted_iota(jnp.int32, by_point.shape, 1)
    mult = jnp.zeros((anterp_ref.shape[1], by_point.shape[1]), F32)
    for leaf in range(0, count, 2):
        maps = jnp.concatenate([anterp_ref[first + leaf], anterp_ref[first + leaf + 1]], 1)
        values = [jnp.where(lane == first + leaf + i, by_point, 0.0) for i in (0, 1)]
        mult = mult + dot(maps, jnp.concatenate(values, 0))
    return mult


def octant_parts(mult, code, child_ref, table_ref):
    devices, slots, nodes = table_ref.shape
    columns = CHILDREN * slots
    by_child = dot_nt(mult.astype(BF16), child_rows(code, columns)).astype(BF16)
    position = lax.broadcasted_iota(jnp.int32, by_child.shape, 1) // slots
    part = jnp.zeros((nodes, columns), F32)
    for child in range(CHILDREN):
        part = part + dot(child_ref[child], jnp.where(position == child, by_child, 0.0))
    part = jnp.sum(part.T.reshape(CHILDREN, slots, nodes), axis=0).astype(BF16)
    for device in range(devices):
        table_ref[device] = part


def downward(tables_ref, counts_ref, trans_ref, code, anterp_ref, child_ref, grouped_s, back_s, maps_ready):
    devices, slots, nodes = tables_ref.shape
    leaves = anterp_ref.shape[0]
    ops = trans_ref.shape[0]
    tables = tables_ref[...].reshape(devices * slots, nodes)
    grouped_s[...] = dot(counts_ref[...], tables).reshape(ops, slots, nodes)

    def translate(i, local):
        for j in range(ops // M2L_LOOP):
            op = i * (ops // M2L_LOOP) + j
            local = local + dot_nt(grouped_s[op].astype(BF16), trans_ref[op])
        return local

    local = lax.fori_loop(0, M2L_LOOP, translate, jnp.zeros((slots, nodes), F32)).astype(BF16)

    def to_children(i, carry):
        for j in range(CHILDREN // L2L_LOOP):
            child = i * (CHILDREN // L2L_LOOP) + j
            back_s[child] = dot(local, child_ref[child])
        return carry

    lax.fori_loop(0, L2L_LOOP, to_children, 0)
    back = back_s[...].reshape(CHILDREN * slots, nodes).astype(BF16)
    pick = child_rows(code, CHILDREN * slots)
    leaf_local = lax.dot_general(pick, back, (((0,), (0,)), ((), ())), preferred_element_type=F32)
    leaf_local = leaf_local.astype(BF16)
    maps_ready()
    far = [dot(leaf_local[leaf : leaf + 1], anterp_ref[leaf]) for leaf in range(leaves)]
    return jnp.concatenate(far, 0)


def update(density, source, far, near):
    potential = FAR_WEIGHT * far + NEAR_WEIGHT * near
    return density + DAMPING * (jnp.tanh(source - potential) - density), potential


def fetch(hbm, vmem, sem):
    copy = pltpu.make_async_copy(hbm, vmem, sem)
    copy.start()
    return copy


def first_kernel(
    pair, octs, q_hbm, child_slot_hbm, parent_hbm, anterp_hbm, child_hbm, table_ref,
    q_s, child_slot_s, parent_s, anterp_s, child_s, sems,
):
    small = [
        fetch(q_hbm, q_s, sems.at[0]),
        fetch(child_slot_hbm, child_slot_s, sems.at[1]),
        fetch(parent_hbm, parent_s, sems.at[2]),
    ]
    chunk = anterp_s.shape[0] // CHUNKS

    def maps(i):
        part = pl.ds(i * chunk, chunk)
        return pltpu.make_async_copy(anterp_hbm.at[part], anterp_s.at[part], sems.at[4 + i])

    for i in range(CHUNKS):
        maps(i).start()
    child = fetch(child_hbm, child_s, sems.at[3])
    for copy in small:
        copy.wait()
    code = leaf_codes(pair, octs, table_ref.shape[1], child_slot_s, parent_s)
    by_point = q_s[...].T.astype(BF16)

    def take(i, mult):
        maps(i).wait()
        return mult + leaf_multipoles(by_point, anterp_s, i * chunk, chunk)

    mult = lax.fori_loop(0, CHUNKS, take, jnp.zeros((anterp_s.shape[1], anterp_s.shape[0]), F32))
    child.wait()
    octant_parts(mult, code, child_s, table_ref)


def later_kernel(
    pair, octs, last, near_ref, tables_ref, counts_ref, source_ref, q_ref, child_slot_ref, parent_ref, trans_ref,
    child_ref, anterp_hbm, new_q_ref, other_out_ref, anterp_s, grouped_s, back_s, sem,
):
    maps = fetch(anterp_hbm, anterp_s, sem)
    code = leaf_codes(pair, octs, tables_ref.shape[1], child_slot_ref, parent_ref)
    far = downward(tables_ref, counts_ref, trans_ref, code, anterp_s, child_ref, grouped_s, back_s, maps.wait)
    new_q, potential = update(q_ref[...], source_ref[...], far, near_ref[...])
    new_q_ref[...] = new_q
    if last:
        other_out_ref[...] = potential
    else:
        mult = leaf_multipoles(new_q.T.astype(BF16), anterp_s, 0, anterp_s.shape[0])
        octant_parts(mult, code, child_ref, other_out_ref)


def counts_kernel(pair, octs, far_list_ref, far_op_ref, counts_ref, rows_s):
    slots, inter = far_list_ref.shape
    rows, columns = counts_ref.shape
    ops = rows // slots
    column = lax.broadcasted_iota(jnp.int32, (columns, inter), 0)
    device, slot = column // slots, column % slots
    octant = (device // 2 * 2 if pair else device - 1) * octs + slot
    op = lax.broadcasted_iota(jnp.int32, (ops, inter), 0)
    for g in range(slots):
        source = jnp.where(octant == far_list_ref[g : g + 1], 1.0, 0.0).astype(BF16)
        chosen = jnp.where(op == far_op_ref[g : g + 1], 1.0, 0.0).astype(BF16)
        rows_s[:, g, :] = dot_nt(chosen, source)
    counts_ref[...] = rows_s[...].reshape(rows, columns).astype(BF16)


def params(mib=4):
    return pltpu.CompilerParams(vmem_limit_bytes=mib << 20)


def swap(array):
    return lax.ppermute(array, "gz", [(0, 1), (1, 0)])


def beside(array, axis, width):
    count = lax.axis_size("gz")
    if count == 2:
        return swap(array)
    length = array.shape[axis]
    up = [(i, i + 1) for i in range(count - 1)]
    down = [(i + 1, i) for i in range(count - 1)]
    after = lax.ppermute(lax.slice_in_dim(array, 0, width, axis=axis), "gz", down)
    before = lax.ppermute(lax.slice_in_dim(array, length - width, length, axis=axis), "gz", up)
    return jnp.concatenate([after, before], axis)


def listed_pairs(near_list, device, pair, rows, halo):
    leaves = near_list.shape[0]
    row = jnp.arange(rows, dtype=jnp.int32)
    if pair:
        leaf = jnp.where(lax.axis_index("gz") == 0, row, leaves - 1 - row)
    else:
        leaf = jnp.where(row < leaves + halo, row, row - rows)
    leaf = leaf + device * leaves
    return jnp.any(near_list[:, :, None] == leaf[None, None, :], axis=1).astype(F32)


def octant_window(array):
    count = lax.axis_size("gz")
    if count == 2:
        other = swap(array)
        low = lax.axis_index("gz") == 0
        return jnp.where(low, jnp.concatenate([array, other], 0), jnp.concatenate([other, array], 0))
    up = [(i, i + 1) for i in range(count - 1)]
    down = [(i + 1, i) for i in range(count - 1)]
    rows = [lax.ppermute(array, "gz", up), array, lax.ppermute(array, "gz", down)]
    rows = jnp.concatenate(rows, 0)
    return jnp.pad(rows, ((0, -rows.shape[0] % 8), (0, 0)))


def shards(
    points, source, density, anterp, child_slot, child_ops, parent, near_list, far_list, far_op, translations
):
    leaves, _, width = points.shape
    octs, inter = far_list.shape
    ops, nodes, _ = translations.shape
    devices = lax.axis_size(AXES)
    pair = lax.axis_size("gz") == 2
    device = lax.axis_index(AXES)
    halo = -(-GHOST // 8) * 8

    child_row, parent_row = child_slot[None, :], parent[None, :]
    slots = -(-(2 if pair else 3) * octs // 8) * 8
    table_shape = jax.ShapeDtypeStruct((devices, slots, nodes), BF16)
    field_shape = jax.ShapeDtypeStruct((leaves, width), F32)
    table = pl.pallas_call(
        functools.partial(first_kernel, pair, octs),
        out_shape=table_shape,
        in_specs=[HBM] * 5,
        out_specs=VMEM,
        scratch_shapes=[
            pltpu.VMEM(density.shape, F32),
            pltpu.VMEM(child_row.shape, jnp.int32),
            pltpu.VMEM(parent_row.shape, jnp.int32),
            pltpu.VMEM(anterp.shape, BF16),
            pltpu.VMEM(child_ops.shape, BF16),
            pltpu.SemaphoreType.DMA((8,)),
        ],
        compiler_params=params(8),
        name="upward_pass",
    )(*map(in_hbm, (density, child_row, parent_row, anterp, child_ops)))

    points, far_list, far_op, near_list, table = lax.optimization_barrier(
        (points, far_list, far_op, near_list, table)
    )
    window = octant_window(far_list * ops + far_op)
    rows = leaves + halo if pair else leaves + 2 * halo
    listed = listed_pairs(near_list, device, pair, rows, halo)
    by_component = points.transpose(1, 0, 2)
    points_other = beside(by_component, 1, halo)

    counts = pl.pallas_call(
        functools.partial(counts_kernel, pair, octs),
        out_shape=jax.ShapeDtypeStruct((ops * slots, devices * slots), BF16),
        in_specs=[VMEM, VMEM],
        out_specs=VMEM,
        scratch_shapes=[pltpu.VMEM((ops, slots, devices * slots), F32)],
        compiler_params=params(4 if pair else 16),
        name="interaction_counts",
    )(window // ops, window % ops)

    density_now = density
    for step in range(ITERS):
        tables = lax.all_to_all(table, AXES, 0, 0, tiled=True)
        q_other = beside(density_now, 0, halo)
        near = near_start(pair, leaves, listed, by_component, points_other, density_now, q_other)
        last = step == ITERS - 1
        density_now, result = pl.pallas_call(
            functools.partial(later_kernel, pair, octs, last),
            out_shape=(field_shape, field_shape if last else table_shape),
            in_specs=[VMEM] * 9 + [HBM],
            out_specs=(VMEM, VMEM),
            scratch_shapes=[
                pltpu.VMEM(anterp.shape, BF16),
                pltpu.VMEM((ops, slots, nodes), F32),
                pltpu.VMEM((CHILDREN, slots, nodes), F32),
                pltpu.SemaphoreType.DMA,
            ],
            compiler_params=params(LATER_MIB),
            name="downward_upward",
        )(near, tables, counts, source, density_now, child_row, parent_row, translations, child_ops, in_hbm(anterp))
        if last:
            potential = result
        else:
            table = result
    return density_now, potential


def solution(mesh):
    rows = P(AXES, None)
    blocks = P(AXES, None, None)
    line = P(AXES)
    in_specs = (blocks, rows, rows, blocks, line, P(), line, rows, rows, rows, P())
    return jax.shard_map(shards, mesh=mesh, in_specs=in_specs, out_specs=(rows, rows), check_vma=False)
```

```python
import functools

import jax
import jax.numpy as jnp
from jax import lax
from jax.experimental import pallas as pl
from jax.experimental.pallas import tpu as pltpu
from jax.sharding import PartitionSpec as P

AXES = ("gx", "gy", "gz")
GHOST = 13
ITERS = 2
CHILDREN = 8

SOFTEN = 0.01
DAMPING = 0.5
FAR_WEIGHT = 0.3
NEAR_WEIGHT = 0.03

BF16 = jnp.bfloat16
F32 = jnp.float32
UNROLL = 16
MATRIX_LEAVES = 8
M2L_LOOP = 2
L2L_LOOP = 2
CHUNKS = 2
LATER_MIB = 6
NT = (((1,), (1,)), ((), ()))
VMEM = pl.BlockSpec(memory_space=pltpu.VMEM)
SMEM = pl.BlockSpec(memory_space=pltpu.SMEM)
HBM = pl.BlockSpec(memory_space=pltpu.HBM)


def in_hbm(array):
    return pltpu.with_memory_space_constraint(array, pltpu.HBM)


def dot(a, b):
    return jnp.dot(a, b, preferred_element_type=F32)


def dot_nt(a, b):
    return lax.dot_general(a, b, NT, preferred_element_type=F32)


def three_parts(x):
    high = x.astype(BF16).astype(F32)
    rest = x - high
    middle = rest.astype(BF16).astype(F32)
    return high, middle, rest - middle


def features(x):
    row = lax.broadcasted_iota(jnp.int32, x.shape, 0)
    high, middle, low = three_parts(x)
    norm = jnp.broadcast_to(jnp.sum(x * x, axis=0, keepdims=True), x.shape)
    nh, nm, nl = three_parts(norm)
    eh, em, el = three_parts(norm + SOFTEN)
    zero = jnp.zeros_like(x)
    last = jnp.where(row < 6, 1.0, 0.0)
    source_norm = jnp.where(row == 0, nh, jnp.where(row == 1, nm, jnp.where(row == 2, nl, last)))
    first = jnp.where(row < 3, 1.0, 0.0)
    target_norm = jnp.where(row == 3, eh, jnp.where(row == 4, em, jnp.where(row == 5, el, first)))
    source = [high, high, middle, middle, high, low, source_norm, zero]
    target = [-2 * high, -2 * middle, -2 * high, -2 * middle, -2 * low, -2 * high, target_norm, zero]
    return jnp.concatenate(source, 0), jnp.concatenate(target, 0)


def coordinates(points_ref, leaf):
    x, y, z = [points_ref[c, pl.ds(leaf, 1), :] for c in range(3)]
    row = lax.broadcasted_iota(jnp.int32, (8, x.shape[1]), 0)
    return jnp.where(row == 0, x, jnp.where(row == 1, y, jnp.where(row == 2, z, 0.0)))


def other_row(pair, low, leaf, leaves):
    return jnp.where(low, leaf, leaves - 1 - leaf) if pair else leaf


def near_part(
    pair, first, count, listed_ref, points_ref, points_other_ref, q_ref, q_other_ref, out_ref,
    source_s, target_s, q_s, ahead_s, back_s,
):
    leaves, width = out_ref.shape
    reach = GHOST + 1
    stop = first + count
    end = stop + GHOST
    low = lax.axis_index("gz") == 0 if pair else True

    def place(i):
        return jnp.where(low, i, leaves - 1 - i) if pair else i

    def own(i, carry):
        leaf = place(i)
        source, target = features(coordinates(points_ref, leaf))
        source_s[i] = source.astype(BF16)
        target_s[i] = target.T.astype(BF16)
        q_s[pl.ds(i, 1), :] = q_ref[pl.ds(leaf, 1), :]
        return carry

    def own_source(i, carry):
        leaf = place(i)
        source_s[i] = features(coordinates(points_ref, leaf))[0].astype(BF16)
        q_s[pl.ds(i, 1), :] = q_ref[pl.ds(leaf, 1), :]
        return carry

    def other(i, carry):
        leaf = other_row(pair, low, i, leaves)
        source_s[leaves + i] = features(coordinates(points_other_ref, leaf))[0].astype(BF16)
        q_s[pl.ds(leaves + i, 1), :] = q_other_ref[pl.ds(leaf, 1), :]
        return carry

    lax.fori_loop(first, stop, own, 0, unroll=16)
    lax.fori_loop(stop, min(end, leaves), own_source, 0, unroll=16)
    lax.fori_loop(0, max(end - leaves, 0), other, 0, unroll=13)

    def target(i, carry):
        rows = target_s[i]
        mine = jnp.broadcast_to(q_s[pl.ds(i, 1), :], (width, width)).T
        acc = jnp.zeros((width, width), F32)
        for d in range(0, reach, 2):
            sources = [source_s[i + d], source_s[i + d + 1]]
            tiles = lax.rsqrt(dot(rows, jnp.concatenate(sources, 1)))
            for part in (0, 1):
                shift = d + part
                tile = tiles[:, part * width : (part + 1) * width]
                acc = acc + tile * (q_s[pl.ds(i + shift, 1), :] * listed_ref[place(i), i + shift])
                if shift:
                    inside = i + shift < leaves
                    weight = listed_ref[place(jnp.minimum(i + shift, leaves - 1)), i]
                    weight = jnp.where(inside, weight, 0.0)
                    back = jnp.sum((tile * mine).reshape(width // 8, 8, width), axis=0)
                    back_s[i + shift, shift - 1] = back * weight
        ahead_s[i] = jnp.sum(acc.T.reshape(width // 8, 8, width), axis=0)
        return carry

    lax.fori_loop(first, stop, target, 0, unroll=min(count, UNROLL))

    if not pair and first == 0:
        halo = q_other_ref.shape[0] // 2
        lax.fori_loop(halo, 2 * halo, other, 0)

        def behind(i, carry):
            acc = jnp.zeros((width, width), F32)
            for j in range(leaves + halo, leaves + 2 * halo):
                tile = lax.rsqrt(dot(target_s[i], source_s[j]))
                acc = acc + tile * (q_s[j : j + 1] * listed_ref[i, j])
            ahead_s[i] = ahead_s[i] + jnp.sum(acc.T.reshape(width // 8, 8, width), axis=0)
            return carry

        lax.fori_loop(0, GHOST, behind, 0)

    for i in range(first, min(end, leaves)):
        terms = [ahead_s[i]] if i < stop else []
        terms += [back_s[i, d - 1] for d in range(1, reach) if first <= i - d < stop]
        total = functools.reduce(jnp.add, terms)
        row = pl.ds(place(i), 1)
        out_ref[row, :] = out_ref[row, :] + jnp.sum(total, axis=0, keepdims=True)


def near_scratch(leaves, rows, width):
    return [
        pltpu.VMEM((rows, 64, width), BF16),
        pltpu.VMEM((leaves, width, 64), BF16),
        pltpu.VMEM((rows, width), F32),
        pltpu.VMEM((leaves, 8, width), F32),
        pltpu.VMEM((leaves + GHOST, GHOST, 8, width), F32),
    ]


def near_kernel(
    pair, count, listed_ref, points_ref, points_other_ref, q_ref, q_other_ref, out_ref,
    source_s, target_s, q_s, ahead_s, back_s,
):
    out_ref[...] = jnp.zeros_like(out_ref)
    near_part(
        pair, 0, count, listed_ref, points_ref, points_other_ref, q_ref, q_other_ref, out_ref,
        source_s, target_s, q_s, ahead_s, back_s,
    )


def near_start(pair, count, listed, points, points_other, q, q_other):
    leaves, width = q.shape
    pairs = count * (GHOST + 1) * width * width
    return pl.pallas_call(
        functools.partial(near_kernel, pair, count),
        out_shape=jax.ShapeDtypeStruct((leaves, width), F32),
        in_specs=[SMEM, VMEM, VMEM, VMEM, VMEM],
        out_specs=VMEM,
        scratch_shapes=near_scratch(leaves, listed.shape[1], width),
        compiler_params=params(6),
        cost_estimate=pl.CostEstimate(flops=pairs * 8192, bytes_accessed=1 << 20, transcendentals=pairs),
        name="near_start",
    )(listed, points, points_other, q, q_other)


def leaf_codes(pair, octs, slots, child_slot_ref, parent_ref):
    device = lax.axis_index(AXES)
    first = (device // 2 * 2 if pair else device - 1) * octs
    return child_slot_ref[...] * slots + (parent_ref[...] - first)


def child_rows(code, rows):
    index = lax.broadcasted_iota(jnp.int32, (rows, code.shape[1]), 0)
    return jnp.where(index == code, 1.0, 0.0).astype(BF16)


def leaf_multipoles(q_ref, anterp_ref, first, count):
    by_point = q_ref[...].T.astype(BF16)
    nodes, leaves = anterp_ref.shape[1], by_point.shape[1]
    lane = lax.broadcasted_iota(jnp.int32, by_point.shape, 1)
    mult = jnp.zeros((nodes, leaves), F32)
    split = count * MATRIX_LEAVES // 16 // 2 * 2
    for leaf in range(0, split, 2):
        maps = jnp.concatenate([anterp_ref[first + leaf], anterp_ref[first + leaf + 1]], 1)
        values = [jnp.where(lane == first + leaf + i, by_point, 0.0) for i in (0, 1)]
        mult = mult + dot(maps, jnp.concatenate(values, 0))
    column = lax.broadcasted_iota(jnp.int32, mult.shape, 1)
    for leaf in range(split, count):
        values = q_ref[pl.ds(first + leaf, 1), :].astype(BF16).astype(F32)
        sums = jnp.sum(anterp_ref[first + leaf].astype(F32) * values, axis=1, keepdims=True)
        mult = jnp.where(column == first + leaf, sums, mult)
    return mult


def octant_parts(mult, code, child_ref, table_ref):
    devices, slots, nodes = table_ref.shape
    columns = CHILDREN * slots
    by_child = dot_nt(mult.astype(BF16), child_rows(code, columns)).astype(BF16)
    position = lax.broadcasted_iota(jnp.int32, by_child.shape, 1) // slots
    part = jnp.zeros((nodes, columns), F32)
    for child in range(CHILDREN):
        part = part + dot(child_ref[child], jnp.where(position == child, by_child, 0.0))
    part = jnp.sum(part.T.reshape(CHILDREN, slots, nodes), axis=0).astype(BF16)
    for device in range(devices):
        table_ref[device] = part


def downward(tables_ref, counts_ref, trans_ref, code, anterp_ref, child_ref, grouped_s, back_s, maps_ready):
    devices, slots, nodes = tables_ref.shape
    leaves = anterp_ref.shape[0]
    ops = trans_ref.shape[0]
    tables = tables_ref[...].reshape(devices * slots, nodes)
    grouped_s[...] = dot(counts_ref[...], tables).reshape(ops, slots, nodes)

    def translate(i, local):
        for j in range(ops // M2L_LOOP):
            op = i * (ops // M2L_LOOP) + j
            local = local + dot_nt(grouped_s[op].astype(BF16), trans_ref[op])
        return local

    local = lax.fori_loop(0, M2L_LOOP, translate, jnp.zeros((slots, nodes), F32)).astype(BF16)

    def to_children(i, carry):
        for j in range(CHILDREN // L2L_LOOP):
            child = i * (CHILDREN // L2L_LOOP) + j
            back_s[child] = dot(local, child_ref[child])
        return carry

    lax.fori_loop(0, L2L_LOOP, to_children, 0)
    back = back_s[...].reshape(CHILDREN * slots, nodes).astype(BF16)
    pick = child_rows(code, CHILDREN * slots)
    leaf_local = lax.dot_general(pick, back, (((0,), (0,)), ((), ())), preferred_element_type=F32)
    leaf_local = leaf_local.astype(BF16)
    maps_ready()
    width = anterp_ref.shape[2]
    far = []
    for leaf in range(0, leaves, 2):
        maps = jnp.concatenate([anterp_ref[leaf], anterp_ref[leaf + 1]], 1)
        both = dot(leaf_local[leaf : leaf + 2], maps)
        far += [both[:1, :width], both[1:, width:]]
    return jnp.concatenate(far, 0)


def update(density, source, far, near):
    potential = FAR_WEIGHT * far + NEAR_WEIGHT * near
    return density + DAMPING * (jnp.tanh(source - potential) - density), potential


def fetch(hbm, vmem, sem):
    copy = pltpu.make_async_copy(hbm, vmem, sem)
    copy.start()
    return copy


def first_kernel(
    pair, octs, q_hbm, child_slot_hbm, parent_hbm, anterp_hbm, child_hbm, table_ref,
    q_s, child_slot_s, parent_s, anterp_s, child_s, sems,
):
    small = [
        fetch(q_hbm, q_s, sems.at[0]),
        fetch(child_slot_hbm, child_slot_s, sems.at[1]),
        fetch(parent_hbm, parent_s, sems.at[2]),
    ]
    chunk = anterp_s.shape[0] // CHUNKS

    def maps(i):
        part = pl.ds(i * chunk, chunk)
        return pltpu.make_async_copy(anterp_hbm.at[part], anterp_s.at[part], sems.at[4 + i])

    for i in range(CHUNKS):
        maps(i).start()
    child = fetch(child_hbm, child_s, sems.at[3])
    for copy in small:
        copy.wait()
    code = leaf_codes(pair, octs, table_ref.shape[1], child_slot_s, parent_s)
    def take(i, mult):
        maps(i).wait()
        return mult + leaf_multipoles(q_s, anterp_s, i * chunk, chunk)

    mult = lax.fori_loop(0, CHUNKS, take, jnp.zeros((anterp_s.shape[1], anterp_s.shape[0]), F32))
    child.wait()
    octant_parts(mult, code, child_s, table_ref)


def later_kernel(
    pair, octs, last, near_ref, tables_ref, counts_ref, source_ref, q_ref, child_slot_ref, parent_ref, trans_ref,
    child_ref, anterp_hbm, new_q_ref, other_out_ref, anterp_s, grouped_s, back_s, sem,
):
    maps = fetch(anterp_hbm, anterp_s, sem)
    code = leaf_codes(pair, octs, tables_ref.shape[1], child_slot_ref, parent_ref)
    far = downward(tables_ref, counts_ref, trans_ref, code, anterp_s, child_ref, grouped_s, back_s, maps.wait)
    new_q, potential = update(q_ref[...], source_ref[...], far, near_ref[...])
    new_q_ref[...] = new_q
    if last:
        other_out_ref[...] = potential
    else:
        mult = leaf_multipoles(new_q_ref, anterp_s, 0, anterp_s.shape[0])
        octant_parts(mult, code, child_ref, other_out_ref)


def counts_kernel(pair, octs, far_list_ref, far_op_ref, counts_ref, rows_s):
    slots, inter = far_list_ref.shape
    rows, columns = counts_ref.shape
    ops = rows // slots
    column = lax.broadcasted_iota(jnp.int32, (columns, inter), 0)
    device, slot = column // slots, column % slots
    octant = (device // 2 * 2 if pair else device - 1) * octs + slot
    op = lax.broadcasted_iota(jnp.int32, (ops, inter), 0)
    for g in range(slots):
        source = jnp.where(octant == far_list_ref[g : g + 1], 1.0, 0.0).astype(BF16)
        chosen = jnp.where(op == far_op_ref[g : g + 1], 1.0, 0.0).astype(BF16)
        rows_s[:, g, :] = dot_nt(chosen, source)
    counts_ref[...] = rows_s[...].reshape(rows, columns).astype(BF16)


def params(mib=4):
    return pltpu.CompilerParams(vmem_limit_bytes=mib << 20)


def swap(array):
    return lax.ppermute(array, "gz", [(0, 1), (1, 0)])


def beside(array, axis, width):
    count = lax.axis_size("gz")
    if count == 2:
        return swap(array)
    length = array.shape[axis]
    up = [(i, i + 1) for i in range(count - 1)]
    down = [(i + 1, i) for i in range(count - 1)]
    after = lax.ppermute(lax.slice_in_dim(array, 0, width, axis=axis), "gz", down)
    before = lax.ppermute(lax.slice_in_dim(array, length - width, length, axis=axis), "gz", up)
    return jnp.concatenate([after, before], axis)


def listed_pairs(near_list, device, pair, rows, halo):
    leaves = near_list.shape[0]
    row = jnp.arange(rows, dtype=jnp.int32)
    if pair:
        leaf = jnp.where(lax.axis_index("gz") == 0, row, leaves - 1 - row)
    else:
        leaf = jnp.where(row < leaves + halo, row, row - rows)
    leaf = leaf + device * leaves
    return jnp.any(near_list[:, :, None] == leaf[None, None, :], axis=1).astype(F32)


def octant_window(array):
    count = lax.axis_size("gz")
    if count == 2:
        other = swap(array)
        low = lax.axis_index("gz") == 0
        return jnp.where(low, jnp.concatenate([array, other], 0), jnp.concatenate([other, array], 0))
    up = [(i, i + 1) for i in range(count - 1)]
    down = [(i + 1, i) for i in range(count - 1)]
    rows = [lax.ppermute(array, "gz", up), array, lax.ppermute(array, "gz", down)]
    rows = jnp.concatenate(rows, 0)
    return jnp.pad(rows, ((0, -rows.shape[0] % 8), (0, 0)))


def shards(
    points, source, density, anterp, child_slot, child_ops, parent, near_list, far_list, far_op, translations
):
    leaves, _, width = points.shape
    octs, inter = far_list.shape
    ops, nodes, _ = translations.shape
    devices = lax.axis_size(AXES)
    pair = lax.axis_size("gz") == 2
    device = lax.axis_index(AXES)
    halo = -(-GHOST // 8) * 8

    child_row, parent_row = child_slot[None, :], parent[None, :]
    slots = -(-(2 if pair else 3) * octs // 8) * 8
    table_shape = jax.ShapeDtypeStruct((devices, slots, nodes), BF16)
    field_shape = jax.ShapeDtypeStruct((leaves, width), F32)
    table = pl.pallas_call(
        functools.partial(first_kernel, pair, octs),
        out_shape=table_shape,
        in_specs=[HBM] * 5,
        out_specs=VMEM,
        scratch_shapes=[
            pltpu.VMEM(density.shape, F32),
            pltpu.VMEM(child_row.shape, jnp.int32),
            pltpu.VMEM(parent_row.shape, jnp.int32),
            pltpu.VMEM(anterp.shape, BF16),
            pltpu.VMEM(child_ops.shape, BF16),
            pltpu.SemaphoreType.DMA((8,)),
        ],
        compiler_params=params(8),
        name="upward_pass",
    )(*map(in_hbm, (density, child_row, parent_row, anterp, child_ops)))

    points, density_sent, far_list, far_op, near_list, table = lax.optimization_barrier(
        (points, density, far_list, far_op, near_list, table)
    )
    window = octant_window(far_list * ops + far_op)
    rows = leaves + halo if pair else leaves + 2 * halo
    listed = listed_pairs(near_list, device, pair, rows, halo)
    by_component = points.transpose(1, 0, 2)
    points_other = beside(by_component, 1, halo)

    counts = pl.pallas_call(
        functools.partial(counts_kernel, pair, octs),
        out_shape=jax.ShapeDtypeStruct((ops * slots, devices * slots), BF16),
        in_specs=[VMEM, VMEM],
        out_specs=VMEM,
        scratch_shapes=[pltpu.VMEM((ops, slots, devices * slots), F32)],
        compiler_params=params(4 if pair else 16),
        name="interaction_counts",
    )(window // ops, window % ops)

    density_now = density
    for step in range(ITERS):
        tables = lax.all_to_all(table, AXES, 0, 0, tiled=True)
        q_other = beside(density_now if step else density_sent, 0, halo)
        near = near_start(pair, leaves, listed, by_component, points_other, density_now, q_other)
        last = step == ITERS - 1
        density_now, result = pl.pallas_call(
            functools.partial(later_kernel, pair, octs, last),
            out_shape=(field_shape, field_shape if last else table_shape),
            in_specs=[VMEM] * 9 + [HBM],
            out_specs=(VMEM, VMEM),
            scratch_shapes=[
                pltpu.VMEM(anterp.shape, BF16),
                pltpu.VMEM((ops, slots, nodes), F32),
                pltpu.VMEM((CHILDREN, slots, nodes), F32),
                pltpu.SemaphoreType.DMA,
            ],
            compiler_params=params(LATER_MIB),
            name="downward_upward",
        )(near, tables, counts, source, density_now, child_row, parent_row, translations, child_ops, in_hbm(anterp))
        if last:
            potential = result
        else:
            table = result
    return density_now, potential


def solution(mesh):
    rows = P(AXES, None)
    blocks = P(AXES, None, None)
    line = P(AXES)
    in_specs = (blocks, rows, rows, blocks, line, P(), line, rows, rows, rows, P())
    return jax.shard_map(shards, mesh=mesh, in_specs=in_specs, out_specs=(rows, rows), check_vma=False)
```

```python
import functools

import jax
import jax.numpy as jnp
from jax import lax
from jax.experimental import pallas as pl
from jax.experimental.pallas import tpu as pltpu
from jax.sharding import PartitionSpec as P

AXES = ("gx", "gy", "gz")
GHOST = 13
ITERS = 2
CHILDREN = 8

SOFTEN = 0.01
DAMPING = 0.5
FAR_WEIGHT = 0.3
NEAR_WEIGHT = 0.03

BF16 = jnp.bfloat16
F32 = jnp.float32
UNROLL = 32
MATRIX_LEAVES = 8
M2L_LOOP = 2
L2L_LOOP = 2
CHUNKS = 2
LATER_MIB = 6
NT = (((1,), (1,)), ((), ()))
VMEM = pl.BlockSpec(memory_space=pltpu.VMEM)
SMEM = pl.BlockSpec(memory_space=pltpu.SMEM)
HBM = pl.BlockSpec(memory_space=pltpu.HBM)


def in_hbm(array):
    return pltpu.with_memory_space_constraint(array, pltpu.HBM)


def dot(a, b):
    return jnp.dot(a, b, preferred_element_type=F32)


def dot_nt(a, b):
    return lax.dot_general(a, b, NT, preferred_element_type=F32)


def three_parts(x):
    high = x.astype(BF16).astype(F32)
    rest = x - high
    middle = rest.astype(BF16).astype(F32)
    return high, middle, rest - middle


def features(x):
    row = lax.broadcasted_iota(jnp.int32, x.shape, 0)
    high, middle, low = three_parts(x)
    norm = jnp.broadcast_to(jnp.sum(x * x, axis=0, keepdims=True), x.shape)
    nh, nm, nl = three_parts(norm)
    eh, em, el = three_parts(norm + SOFTEN)
    zero = jnp.zeros_like(x)
    last = jnp.where(row < 6, 1.0, 0.0)
    source_norm = jnp.where(row == 0, nh, jnp.where(row == 1, nm, jnp.where(row == 2, nl, last)))
    first = jnp.where(row < 3, 1.0, 0.0)
    target_norm = jnp.where(row == 3, eh, jnp.where(row == 4, em, jnp.where(row == 5, el, first)))
    source = [high, high, middle, middle, high, low, source_norm, zero]
    target = [-2 * high, -2 * middle, -2 * high, -2 * middle, -2 * low, -2 * high, target_norm, zero]
    return jnp.concatenate(source, 0), jnp.concatenate(target, 0)


def coordinates(points_ref, leaf, stride):
    x, y, z = [points_ref[pl.ds(c * stride + leaf, 1), :] for c in range(3)]
    row = lax.broadcasted_iota(jnp.int32, (8, x.shape[1]), 0)
    return jnp.where(row == 0, x, jnp.where(row == 1, y, jnp.where(row == 2, z, 0.0)))


def other_row(pair, low, leaf, leaves):
    return jnp.where(low, leaf, leaves - 1 - leaf) if pair else leaf


def near_part(
    pair, first, count, others, q_row, listed_ref, points_ref, points_other_ref, q_ref, q_other_ref, out_ref,
    source_s, target_s, q_s, ahead_s, back_s,
):
    leaves, width = out_ref.shape
    reach = GHOST + 1
    stop = first + count
    end = stop + GHOST
    low = lax.axis_index("gz") == 0 if pair else True

    def place(i):
        return jnp.where(low, i, leaves - 1 - i) if pair else i

    def own(i, carry):
        leaf = place(i)
        source, target = features(coordinates(points_ref, leaf, leaves))
        source_s[i] = source.astype(BF16)
        target_s[i] = target.T.astype(BF16)
        q_s[pl.ds(i, 1), :] = q_ref[pl.ds(leaf, 1), :]
        return carry

    def own_source(i, carry):
        leaf = place(i)
        source_s[i] = features(coordinates(points_ref, leaf, leaves))[0].astype(BF16)
        q_s[pl.ds(i, 1), :] = q_ref[pl.ds(leaf, 1), :]
        return carry

    def other(i, carry):
        leaf = other_row(pair, low, i, leaves)
        source_s[leaves + i] = features(coordinates(points_other_ref, leaf, others))[0].astype(BF16)
        q_s[pl.ds(leaves + i, 1), :] = q_other_ref[pl.ds(q_row + leaf, 1), :]
        return carry

    lax.fori_loop(first, stop, own, 0, unroll=16)
    lax.fori_loop(stop, min(end, leaves), own_source, 0, unroll=16)
    lax.fori_loop(0, max(end - leaves, 0), other, 0, unroll=13)

    def target(i, carry):
        rows = target_s[i]
        mine = jnp.broadcast_to(q_s[pl.ds(i, 1), :], (width, width)).T
        acc = jnp.zeros((width, width), F32)
        for d in range(0, reach, 2):
            sources = [source_s[i + d], source_s[i + d + 1]]
            tiles = lax.rsqrt(dot(rows, jnp.concatenate(sources, 1)))
            for part in (0, 1):
                shift = d + part
                tile = tiles[:, part * width : (part + 1) * width]
                acc = acc + tile * (q_s[pl.ds(i + shift, 1), :] * listed_ref[place(i), i + shift])
                if shift:
                    inside = i + shift < leaves
                    weight = listed_ref[place(jnp.minimum(i + shift, leaves - 1)), i]
                    weight = jnp.where(inside, weight, 0.0)
                    back = jnp.sum((tile * mine).reshape(width // 8, 8, width), axis=0)
                    back_s[i + shift, shift - 1] = back * weight
        ahead_s[i] = jnp.sum(acc.T.reshape(width // 8, 8, width), axis=0)
        return carry

    lax.fori_loop(first, stop, target, 0, unroll=min(count, UNROLL))

    if not pair and first == 0:
        halo = others // 2
        lax.fori_loop(halo, 2 * halo, other, 0)

        def behind(i, carry):
            acc = jnp.zeros((width, width), F32)
            for j in range(leaves + halo, leaves + 2 * halo):
                tile = lax.rsqrt(dot(target_s[i], source_s[j]))
                acc = acc + tile * (q_s[j : j + 1] * listed_ref[i, j])
            ahead_s[i] = ahead_s[i] + jnp.sum(acc.T.reshape(width // 8, 8, width), axis=0)
            return carry

        lax.fori_loop(0, GHOST, behind, 0)

    for i in range(first, min(end, leaves)):
        terms = [ahead_s[i]] if i < stop else []
        terms += [back_s[i, d - 1] for d in range(1, reach) if first <= i - d < stop]
        total = functools.reduce(jnp.add, terms)
        row = pl.ds(place(i), 1)
        out_ref[row, :] = out_ref[row, :] + jnp.sum(total, axis=0, keepdims=True)


def near_scratch(leaves, rows, width):
    return [
        pltpu.VMEM((rows, 64, width), BF16),
        pltpu.VMEM((leaves, width, 64), BF16),
        pltpu.VMEM((rows, width), F32),
        pltpu.VMEM((leaves, 8, width), F32),
        pltpu.VMEM((leaves + GHOST, GHOST, 8, width), F32),
    ]


def near_kernel(
    pair, count, others, q_row, listed_ref, points_ref, points_other_ref, q_ref, q_other_ref, out_ref,
    source_s, target_s, q_s, ahead_s, back_s,
):
    out_ref[...] = jnp.zeros_like(out_ref)
    near_part(
        pair, 0, count, others, q_row, listed_ref, points_ref, points_other_ref, q_ref, q_other_ref, out_ref,
        source_s, target_s, q_s, ahead_s, back_s,
    )


def near_start(pair, count, others, q_row, listed, points, points_other, q, q_other):
    leaves, width = q.shape
    pairs = count * (GHOST + 1) * width * width
    return pl.pallas_call(
        functools.partial(near_kernel, pair, count, others, q_row),
        out_shape=jax.ShapeDtypeStruct((leaves, width), F32),
        in_specs=[SMEM, VMEM, VMEM, VMEM, VMEM],
        out_specs=VMEM,
        scratch_shapes=near_scratch(leaves, listed.shape[1], width),
        compiler_params=params(8),
        cost_estimate=pl.CostEstimate(flops=pairs * 8192, bytes_accessed=1 << 20, transcendentals=pairs),
        name="near_start",
    )(listed, points, points_other, q, q_other)


def leaf_codes(pair, octs, slots, child_slot_ref, parent_ref):
    device = lax.axis_index(AXES)
    first = (device // 2 * 2 if pair else device - 1) * octs
    return child_slot_ref[...] * slots + (parent_ref[...] - first)


def child_rows(code, rows):
    index = lax.broadcasted_iota(jnp.int32, (rows, code.shape[1]), 0)
    return jnp.where(index == code, 1.0, 0.0).astype(BF16)


def leaf_multipoles(q_ref, anterp_ref, first, count):
    by_point = q_ref[...].T.astype(BF16)
    nodes, leaves = anterp_ref.shape[1], by_point.shape[1]
    lane = lax.broadcasted_iota(jnp.int32, by_point.shape, 1)
    mult = jnp.zeros((nodes, leaves), F32)
    split = count * MATRIX_LEAVES // 16 // 2 * 2
    for leaf in range(0, split, 2):
        maps = jnp.concatenate([anterp_ref[first + leaf], anterp_ref[first + leaf + 1]], 1)
        values = [jnp.where(lane == first + leaf + i, by_point, 0.0) for i in (0, 1)]
        mult = mult + dot(maps, jnp.concatenate(values, 0))
    column = lax.broadcasted_iota(jnp.int32, mult.shape, 1)
    for leaf in range(split, count):
        values = q_ref[pl.ds(first + leaf, 1), :].astype(BF16).astype(F32)
        sums = jnp.sum(anterp_ref[first + leaf].astype(F32) * values, axis=1, keepdims=True)
        mult = jnp.where(column == first + leaf, sums, mult)
    return mult


def octant_parts(mult, code, child_ref, table_ref):
    devices, slots, nodes = table_ref.shape
    by_child = dot_nt(mult.astype(BF16), child_rows(code, CHILDREN * slots)).T.astype(BF16)
    part = jnp.zeros((slots, nodes), F32)
    for child in range(CHILDREN):
        part = part + dot_nt(by_child[child * slots : (child + 1) * slots], child_ref[child])
    part = part.astype(BF16)
    for device in range(devices):
        table_ref[device] = part


def downward(tables_ref, counts_ref, trans_ref, code, anterp_ref, child_ref, grouped_s, back_s, maps_ready):
    devices, slots, nodes = tables_ref.shape
    leaves = anterp_ref.shape[0]
    ops = trans_ref.shape[0]
    tables = tables_ref[...].reshape(devices * slots, nodes)
    grouped_s[...] = dot(counts_ref[...], tables).reshape(ops, slots, nodes)

    def translate(i, local):
        for j in range(ops // M2L_LOOP):
            op = i * (ops // M2L_LOOP) + j
            local = local + dot_nt(grouped_s[op].astype(BF16), trans_ref[op])
        return local

    local = lax.fori_loop(0, M2L_LOOP, translate, jnp.zeros((slots, nodes), F32)).astype(BF16)

    def to_children(i, carry):
        for j in range(CHILDREN // L2L_LOOP):
            child = i * (CHILDREN // L2L_LOOP) + j
            back_s[child] = dot(local, child_ref[child])
        return carry

    lax.fori_loop(0, L2L_LOOP, to_children, 0)
    back = back_s[...].reshape(CHILDREN * slots, nodes).astype(BF16)
    pick = child_rows(code, CHILDREN * slots)
    leaf_local = lax.dot_general(pick, back, (((0,), (0,)), ((), ())), preferred_element_type=F32)
    leaf_local = leaf_local.astype(BF16)
    maps_ready()
    width = anterp_ref.shape[2]
    far = []
    for leaf in range(0, leaves, 2):
        maps = jnp.concatenate([anterp_ref[leaf], anterp_ref[leaf + 1]], 1)
        both = dot(leaf_local[leaf : leaf + 2], maps)
        far += [both[:1, :width], both[1:, width:]]
    return jnp.concatenate(far, 0)


def update(density, source, far, near):
    potential = FAR_WEIGHT * far + NEAR_WEIGHT * near
    return density + DAMPING * (jnp.tanh(source - potential) - density), potential


def fetch(hbm, vmem, sem):
    copy = pltpu.make_async_copy(hbm, vmem, sem)
    copy.start()
    return copy


def first_kernel(
    pair, octs, q_hbm, child_slot_hbm, parent_hbm, anterp_hbm, child_hbm, table_ref,
    q_s, child_slot_s, parent_s, anterp_s, child_s, sems,
):
    small = [
        fetch(q_hbm, q_s, sems.at[0]),
        fetch(child_slot_hbm, child_slot_s, sems.at[1]),
        fetch(parent_hbm, parent_s, sems.at[2]),
    ]
    chunk = anterp_s.shape[0] // CHUNKS

    def maps(i):
        part = pl.ds(i * chunk, chunk)
        return pltpu.make_async_copy(anterp_hbm.at[part], anterp_s.at[part], sems.at[4 + i])

    for i in range(CHUNKS):
        maps(i).start()
    child = fetch(child_hbm, child_s, sems.at[3])
    for copy in small:
        copy.wait()
    code = leaf_codes(pair, octs, table_ref.shape[1], child_slot_s, parent_s)
    def take(i, mult):
        maps(i).wait()
        return mult + leaf_multipoles(q_s, anterp_s, i * chunk, chunk)

    mult = lax.fori_loop(0, CHUNKS, take, jnp.zeros((anterp_s.shape[1], anterp_s.shape[0]), F32))
    child.wait()
    octant_parts(mult, code, child_s, table_ref)


def later_kernel(
    pair, octs, last, near_ref, tables_ref, counts_ref, source_ref, q_ref, child_slot_ref, parent_ref, trans_ref,
    child_ref, anterp_hbm, new_q_ref, other_out_ref, anterp_s, grouped_s, back_s, sem,
):
    maps = fetch(anterp_hbm, anterp_s, sem)
    code = leaf_codes(pair, octs, tables_ref.shape[1], child_slot_ref, parent_ref)
    far = downward(tables_ref, counts_ref, trans_ref, code, anterp_s, child_ref, grouped_s, back_s, maps.wait)
    new_q, potential = update(q_ref[...], source_ref[...], far, near_ref[...])
    new_q_ref[...] = new_q
    if last:
        other_out_ref[...] = potential
    else:
        mult = leaf_multipoles(new_q_ref, anterp_s, 0, anterp_s.shape[0])
        octant_parts(mult, code, child_ref, other_out_ref)


def counts_kernel(pair, octs, far_list_ref, far_op_ref, other_ref, counts_ref, rows_s):
    own, inter = far_list_ref.shape
    rows, columns = counts_ref.shape
    ops, slots, _ = rows_s.shape

    column = lax.broadcasted_iota(jnp.int32, (columns, inter), 0)
    device, slot = column // slots, column % slots
    octant = (device // 2 * 2 if pair else device - 1) * octs + slot
    op = lax.broadcasted_iota(jnp.int32, (ops, inter), 0)

    def count(g, far_list, far_op):
        source = jnp.where(octant == far_list, 1.0, 0.0).astype(BF16)
        chosen = jnp.where(op == far_op, 1.0, 0.0).astype(BF16)
        rows_s[:, pl.ds(g, 1), :] = dot_nt(chosen, source).reshape(ops, 1, columns)

    low = lax.axis_index("gz") == 0
    for g in range(own):
        count(jnp.where(low, g, octs + g) if pair else g, far_list_ref[g : g + 1], far_op_ref[g : g + 1])
    if pair:
        for g in range(octs):
            row = other_ref[g : g + 1]
            count(jnp.where(low, octs + g, g), row // ops, row % ops)
    counts_ref[...] = rows_s[...].reshape(rows, columns).astype(BF16)


def params(mib=4):
    return pltpu.CompilerParams(vmem_limit_bytes=mib << 20)


def swap(array):
    return lax.ppermute(array, "gz", [(0, 1), (1, 0)])


def beside(array, axis, width):
    count = lax.axis_size("gz")
    if count == 2:
        return swap(array)
    length = array.shape[axis]
    up = [(i, i + 1) for i in range(count - 1)]
    down = [(i + 1, i) for i in range(count - 1)]
    after = lax.ppermute(lax.slice_in_dim(array, 0, width, axis=axis), "gz", down)
    before = lax.ppermute(lax.slice_in_dim(array, length - width, length, axis=axis), "gz", up)
    return jnp.concatenate([after, before], axis)


def listed_pairs(near_list, device, pair, rows, halo):
    leaves = near_list.shape[0]
    row = jnp.arange(rows, dtype=jnp.int32)
    if pair:
        leaf = jnp.where(lax.axis_index("gz") == 0, row, leaves - 1 - row)
    else:
        leaf = jnp.where(row < leaves + halo, row, row - rows)
    leaf = leaf + device * leaves
    leaf = jnp.where(leaf < 0, -2, leaf)
    return jnp.any(near_list[:, :, None] == leaf[None, None, :], axis=1).astype(F32)


def octant_window(array):
    count = lax.axis_size("gz")
    up = [(i, i + 1) for i in range(count - 1)]
    down = [(i + 1, i) for i in range(count - 1)]
    rows = [lax.ppermute(array, "gz", up), array, lax.ppermute(array, "gz", down)]
    rows = jnp.concatenate(rows, 0)
    return jnp.pad(rows, ((0, -rows.shape[0] % 8), (0, 0)))


def shards(
    points, source, density, anterp, child_slot, child_ops, parent, near_list, far_list, far_op, translations
):
    leaves, _, width = points.shape
    octs, inter = far_list.shape
    ops, nodes, _ = translations.shape
    devices = lax.axis_size(AXES)
    pair = lax.axis_size("gz") == 2
    device = lax.axis_index(AXES)
    halo = -(-GHOST // 8) * 8

    child_row, parent_row = child_slot[None, :], parent[None, :]
    slots = -(-(2 if pair else 3) * octs // 8) * 8
    table_shape = jax.ShapeDtypeStruct((devices, slots, nodes), BF16)
    field_shape = jax.ShapeDtypeStruct((leaves, width), F32)
    table = pl.pallas_call(
        functools.partial(first_kernel, pair, octs),
        out_shape=table_shape,
        in_specs=[HBM] * 5,
        out_specs=VMEM,
        scratch_shapes=[
            pltpu.VMEM(density.shape, F32),
            pltpu.VMEM(child_row.shape, jnp.int32),
            pltpu.VMEM(parent_row.shape, jnp.int32),
            pltpu.VMEM(anterp.shape, BF16),
            pltpu.VMEM(child_ops.shape, BF16),
            pltpu.SemaphoreType.DMA((8,)),
        ],
        compiler_params=params(8),
        name="upward_pass",
    )(*map(in_hbm, (density, child_row, parent_row, anterp, child_ops)))

    points, density_sent, far_list, far_op, near_list, table = lax.optimization_barrier(
        (points, density, far_list, far_op, near_list, table)
    )
    rows = leaves + halo if pair else leaves + 2 * halo
    listed = listed_pairs(near_list, device, pair, rows, halo)
    own_points = points.transpose(1, 0, 2).reshape(3 * leaves, width)
    if pair:
        others, first_q_row = leaves, 3 * leaves
        lists = (far_list, far_op, swap(far_list * ops + far_op))
        points_other = first_q_other = swap(jnp.concatenate([own_points, density_sent], 0))
    else:
        others, first_q_row = 2 * halo, 0
        points_other = beside(own_points.reshape(3, leaves, width), 1, halo).reshape(3 * others, width)
        first_q_other = beside(density_sent, 0, halo)
        window = octant_window(far_list * ops + far_op)
        lists = (window // ops, window % ops, window)

    counts = pl.pallas_call(
        functools.partial(counts_kernel, pair, octs),
        out_shape=jax.ShapeDtypeStruct((ops * slots, devices * slots), BF16),
        in_specs=[VMEM, VMEM, VMEM],
        out_specs=VMEM,
        scratch_shapes=[pltpu.VMEM((ops, slots, devices * slots), F32)],
        compiler_params=params(4 if pair else 16),
        name="interaction_counts",
    )(*lists)

    density_now = density
    for step in range(ITERS):
        tables = lax.all_to_all(table, AXES, 0, 0, tiled=True)
        q_other, q_row = (beside(density_now, 0, halo), 0) if step else (first_q_other, first_q_row)
        near = near_start(pair, leaves, others, q_row, listed, own_points, points_other, density_now, q_other)
        last = step == ITERS - 1
        density_now, result = pl.pallas_call(
            functools.partial(later_kernel, pair, octs, last),
            out_shape=(field_shape, field_shape if last else table_shape),
            in_specs=[VMEM] * 9 + [HBM],
            out_specs=(VMEM, VMEM),
            scratch_shapes=[
                pltpu.VMEM(anterp.shape, BF16),
                pltpu.VMEM((ops, slots, nodes), F32),
                pltpu.VMEM((CHILDREN, slots, nodes), F32),
                pltpu.SemaphoreType.DMA,
            ],
            compiler_params=params(LATER_MIB),
            name="downward_upward",
        )(near, tables, counts, source, density_now, child_row, parent_row, translations, child_ops, in_hbm(anterp))
        if last:
            potential = result
        else:
            table = result
    return density_now, potential


def solution(mesh):
    rows = P(AXES, None)
    blocks = P(AXES, None, None)
    line = P(AXES)
    in_specs = (blocks, rows, rows, blocks, line, P(), line, rows, rows, rows, P())
    return jax.shard_map(shards, mesh=mesh, in_specs=in_specs, out_specs=(rows, rows), check_vma=False)
```

```python
import functools

import jax
import jax.numpy as jnp
from jax import lax
from jax.experimental import pallas as pl
from jax.experimental.pallas import tpu as pltpu
from jax.sharding import PartitionSpec as P

AXES = ("gx", "gy", "gz")
GHOST = 13
ITERS = 2
CHILDREN = 8

SOFTEN = 0.01
DAMPING = 0.5
FAR_WEIGHT = 0.3
NEAR_WEIGHT = 0.03

BF16 = jnp.bfloat16
F32 = jnp.float32
UNROLL = 32
MATRIX_LEAVES = 8
M2L_LOOP = 2
L2L_LOOP = 2
CHUNKS = 2
LATER_MIB = 6
NT = (((1,), (1,)), ((), ()))
VMEM = pl.BlockSpec(memory_space=pltpu.VMEM)
SMEM = pl.BlockSpec(memory_space=pltpu.SMEM)
HBM = pl.BlockSpec(memory_space=pltpu.HBM)


def in_hbm(array):
    return pltpu.with_memory_space_constraint(array, pltpu.HBM)


def dot(a, b):
    return jnp.dot(a, b, preferred_element_type=F32)


def dot_nt(a, b):
    return lax.dot_general(a, b, NT, preferred_element_type=F32)


def three_parts(x):
    high = x.astype(BF16).astype(F32)
    rest = x - high
    middle = rest.astype(BF16).astype(F32)
    return high, middle, rest - middle


def features(x):
    row = lax.broadcasted_iota(jnp.int32, x.shape, 0)
    high, middle, low = three_parts(x)
    norm = jnp.broadcast_to(jnp.sum(x * x, axis=0, keepdims=True), x.shape)
    nh, nm, nl = three_parts(norm)
    eh, em, el = three_parts(norm + SOFTEN)
    zero = jnp.zeros_like(x)
    last = jnp.where(row < 6, 1.0, 0.0)
    source_norm = jnp.where(row == 0, nh, jnp.where(row == 1, nm, jnp.where(row == 2, nl, last)))
    first = jnp.where(row < 3, 1.0, 0.0)
    target_norm = jnp.where(row == 3, eh, jnp.where(row == 4, em, jnp.where(row == 5, el, first)))
    source = [high, high, middle, middle, high, low, source_norm, zero]
    target = [-2 * high, -2 * middle, -2 * high, -2 * middle, -2 * low, -2 * high, target_norm, zero]
    return jnp.concatenate(source, 0), jnp.concatenate(target, 0)


def coordinates(points_ref, leaf, stride):
    x, y, z = [points_ref[pl.ds(c * stride + leaf, 1), :] for c in range(3)]
    row = lax.broadcasted_iota(jnp.int32, (8, x.shape[1]), 0)
    return jnp.where(row == 0, x, jnp.where(row == 1, y, jnp.where(row == 2, z, 0.0)))


def other_row(pair, low, leaf, leaves):
    return jnp.where(low, leaf, leaves - 1 - leaf) if pair else leaf


def near_part(
    pair, first, count, others, q_row, listed_ref, points_ref, points_other_ref, q_ref, q_other_ref, out_ref,
    source_s, target_s, q_s, ahead_s, back_s,
):
    leaves, width = out_ref.shape
    reach = GHOST + 1
    stop = first + count
    end = stop + GHOST
    low = lax.axis_index("gz") == 0 if pair else True

    def place(i):
        return jnp.where(low, i, leaves - 1 - i) if pair else i

    def own(i, carry):
        leaf = place(i)
        source, target = features(coordinates(points_ref, leaf, leaves))
        source_s[i] = source.astype(BF16)
        target_s[i] = target.T.astype(BF16)
        q_s[pl.ds(i, 1), :] = q_ref[pl.ds(leaf, 1), :]
        return carry

    def own_source(i, carry):
        leaf = place(i)
        source_s[i] = features(coordinates(points_ref, leaf, leaves))[0].astype(BF16)
        q_s[pl.ds(i, 1), :] = q_ref[pl.ds(leaf, 1), :]
        return carry

    def other(i, carry):
        leaf = other_row(pair, low, i, leaves)
        source_s[leaves + i] = features(coordinates(points_other_ref, leaf, others))[0].astype(BF16)
        first_q, q_rows = q_row
        q_s[pl.ds(leaves + i, 1), :] = q_other_ref[pl.ds(first_q + other_row(pair, low, i, q_rows), 1), :]
        return carry

    lax.fori_loop(first, stop, own, 0, unroll=16)
    lax.fori_loop(stop, min(end, leaves), own_source, 0, unroll=16)
    lax.fori_loop(0, max(end - leaves, 0), other, 0, unroll=13)

    def target(i, carry):
        rows = target_s[i]
        mine = jnp.broadcast_to(q_s[pl.ds(i, 1), :], (width, width)).T
        acc = jnp.zeros((width, width), F32)
        for d in range(0, reach, 2):
            sources = [source_s[i + d], source_s[i + d + 1]]
            tiles = lax.rsqrt(dot(rows, jnp.concatenate(sources, 1)))
            for part in (0, 1):
                shift = d + part
                tile = tiles[:, part * width : (part + 1) * width]
                acc = acc + tile * (q_s[pl.ds(i + shift, 1), :] * listed_ref[place(i), i + shift])
                if shift:
                    inside = i + shift < leaves
                    weight = listed_ref[place(jnp.minimum(i + shift, leaves - 1)), i]
                    weight = jnp.where(inside, weight, 0.0)
                    back = jnp.sum((tile * mine).reshape(width // 8, 8, width), axis=0)
                    back_s[i + shift, shift - 1] = back * weight
        ahead_s[i] = jnp.sum(acc.T.reshape(width // 8, 8, width), axis=0)
        return carry

    lax.fori_loop(first, stop, target, 0, unroll=min(count, UNROLL))

    if not pair and first == 0:
        halo = others // 2
        lax.fori_loop(halo, 2 * halo, other, 0)

        def behind(i, carry):
            acc = jnp.zeros((width, width), F32)
            for j in range(leaves + halo, leaves + 2 * halo):
                tile = lax.rsqrt(dot(target_s[i], source_s[j]))
                acc = acc + tile * (q_s[j : j + 1] * listed_ref[i, j])
            ahead_s[i] = ahead_s[i] + jnp.sum(acc.T.reshape(width // 8, 8, width), axis=0)
            return carry

        lax.fori_loop(0, GHOST, behind, 0)

    for i in range(first, min(end, leaves)):
        terms = [ahead_s[i]] if i < stop else []
        terms += [back_s[i, d - 1] for d in range(1, reach) if first <= i - d < stop]
        total = functools.reduce(jnp.add, terms)
        row = pl.ds(place(i), 1)
        out_ref[row, :] = out_ref[row, :] + jnp.sum(total, axis=0, keepdims=True)


def near_scratch(leaves, rows, width):
    return [
        pltpu.VMEM((rows, 64, width), BF16),
        pltpu.VMEM((leaves, width, 64), BF16),
        pltpu.VMEM((rows, width), F32),
        pltpu.VMEM((leaves, 8, width), F32),
        pltpu.VMEM((leaves + GHOST, GHOST, 8, width), F32),
    ]


def near_kernel(
    pair, count, others, q_row, listed_ref, points_ref, points_other_ref, q_ref, q_other_ref, out_ref,
    source_s, target_s, q_s, ahead_s, back_s,
):
    out_ref[...] = jnp.zeros_like(out_ref)
    near_part(
        pair, 0, count, others, q_row, listed_ref, points_ref, points_other_ref, q_ref, q_other_ref, out_ref,
        source_s, target_s, q_s, ahead_s, back_s,
    )


def near_start(pair, count, others, q_row, listed, points, points_other, q, q_other):
    leaves, width = q.shape
    pairs = count * (GHOST + 1) * width * width
    return pl.pallas_call(
        functools.partial(near_kernel, pair, count, others, q_row),
        out_shape=jax.ShapeDtypeStruct((leaves, width), F32),
        in_specs=[SMEM, VMEM, VMEM, VMEM, VMEM],
        out_specs=VMEM,
        scratch_shapes=near_scratch(leaves, listed.shape[1], width),
        compiler_params=params(8),
        cost_estimate=pl.CostEstimate(flops=pairs * 8192, bytes_accessed=1 << 20, transcendentals=pairs),
        name="near_start",
    )(listed, points, points_other, q, q_other)


def leaf_codes(pair, octs, slots, child_slot_ref, parent_ref):
    device = lax.axis_index(AXES)
    first = (device // 2 * 2 if pair else device - 1) * octs
    return child_slot_ref[...] * slots + (parent_ref[...] - first)


def child_rows(code, rows):
    index = lax.broadcasted_iota(jnp.int32, (rows, code.shape[1]), 0)
    return jnp.where(index == code, 1.0, 0.0).astype(BF16)


def leaf_multipoles(q_ref, anterp_ref, first, count):
    by_point = q_ref[...].T.astype(BF16)
    nodes, leaves = anterp_ref.shape[1], by_point.shape[1]
    lane = lax.broadcasted_iota(jnp.int32, by_point.shape, 1)
    mult = jnp.zeros((nodes, leaves), F32)
    split = count * MATRIX_LEAVES // 16 // 2 * 2
    for leaf in range(0, split, 2):
        maps = jnp.concatenate([anterp_ref[first + leaf], anterp_ref[first + leaf + 1]], 1)
        values = [jnp.where(lane == first + leaf + i, by_point, 0.0) for i in (0, 1)]
        mult = mult + dot(maps, jnp.concatenate(values, 0))
    column = lax.broadcasted_iota(jnp.int32, mult.shape, 1)
    for leaf in range(split, count):
        values = q_ref[pl.ds(first + leaf, 1), :].astype(BF16).astype(F32)
        sums = jnp.sum(anterp_ref[first + leaf].astype(F32) * values, axis=1, keepdims=True)
        mult = jnp.where(column == first + leaf, sums, mult)
    return mult


def octant_parts(mult, code, child_ref, table_ref):
    devices, slots, nodes = table_ref.shape
    by_child = dot_nt(mult.astype(BF16), child_rows(code, CHILDREN * slots)).T.astype(BF16)
    part = jnp.zeros((slots, nodes), F32)
    for child in range(CHILDREN):
        part = part + dot_nt(by_child[child * slots : (child + 1) * slots], child_ref[child])
    part = part.astype(BF16)
    for device in range(devices):
        table_ref[device] = part


def downward(tables_ref, counts_ref, trans_ref, code, anterp_ref, child_ref, grouped_s, back_s, maps_ready):
    devices, slots, nodes = tables_ref.shape
    leaves = anterp_ref.shape[0]
    ops = trans_ref.shape[0]
    tables = tables_ref[...].reshape(devices * slots, nodes)
    grouped_s[...] = dot(counts_ref[...], tables).reshape(ops, slots, nodes)

    def translate(i, local):
        for j in range(ops // M2L_LOOP):
            op = i * (ops // M2L_LOOP) + j
            local = local + dot_nt(grouped_s[op].astype(BF16), trans_ref[op])
        return local

    local = lax.fori_loop(0, M2L_LOOP, translate, jnp.zeros((slots, nodes), F32)).astype(BF16)

    def to_children(i, carry):
        for j in range(CHILDREN // L2L_LOOP):
            child = i * (CHILDREN // L2L_LOOP) + j
            back_s[child] = dot(local, child_ref[child])
        return carry

    lax.fori_loop(0, L2L_LOOP, to_children, 0)
    back = back_s[...].reshape(CHILDREN * slots, nodes).astype(BF16)
    pick = child_rows(code, CHILDREN * slots)
    leaf_local = lax.dot_general(pick, back, (((0,), (0,)), ((), ())), preferred_element_type=F32)
    leaf_local = leaf_local.astype(BF16)
    maps_ready()
    width = anterp_ref.shape[2]
    far = []
    for leaf in range(0, leaves, 2):
        maps = jnp.concatenate([anterp_ref[leaf], anterp_ref[leaf + 1]], 1)
        both = dot(leaf_local[leaf : leaf + 2], maps)
        far += [both[:1, :width], both[1:, width:]]
    return jnp.concatenate(far, 0)


def update(density, source, far, near):
    potential = FAR_WEIGHT * far + NEAR_WEIGHT * near
    return density + DAMPING * (jnp.tanh(source - potential) - density), potential


def fetch(hbm, vmem, sem):
    copy = pltpu.make_async_copy(hbm, vmem, sem)
    copy.start()
    return copy


def first_kernel(
    pair, octs, q_hbm, child_slot_hbm, parent_hbm, anterp_hbm, child_hbm, table_ref,
    q_s, child_slot_s, parent_s, anterp_s, child_s, sems,
):
    small = [
        fetch(q_hbm, q_s, sems.at[0]),
        fetch(child_slot_hbm, child_slot_s, sems.at[1]),
        fetch(parent_hbm, parent_s, sems.at[2]),
    ]
    chunk = anterp_s.shape[0] // CHUNKS

    def maps(i):
        part = pl.ds(i * chunk, chunk)
        return pltpu.make_async_copy(anterp_hbm.at[part], anterp_s.at[part], sems.at[4 + i])

    for i in range(CHUNKS):
        maps(i).start()
    child = fetch(child_hbm, child_s, sems.at[3])
    for copy in small:
        copy.wait()
    code = leaf_codes(pair, octs, table_ref.shape[1], child_slot_s, parent_s)
    def take(i, mult):
        maps(i).wait()
        return mult + leaf_multipoles(q_s, anterp_s, i * chunk, chunk)

    mult = lax.fori_loop(0, CHUNKS, take, jnp.zeros((anterp_s.shape[1], anterp_s.shape[0]), F32))
    child.wait()
    octant_parts(mult, code, child_s, table_ref)


def later_kernel(
    pair, octs, last, near_ref, tables_ref, counts_ref, source_ref, q_ref, child_slot_ref, parent_ref, trans_ref,
    child_ref, anterp_hbm, new_q_ref, other_out_ref, anterp_s, grouped_s, back_s, sem,
):
    maps = fetch(anterp_hbm, anterp_s, sem)
    code = leaf_codes(pair, octs, tables_ref.shape[1], child_slot_ref, parent_ref)
    far = downward(tables_ref, counts_ref, trans_ref, code, anterp_s, child_ref, grouped_s, back_s, maps.wait)
    new_q, potential = update(q_ref[...], source_ref[...], far, near_ref[...])
    new_q_ref[...] = new_q
    if last:
        other_out_ref[...] = potential
    else:
        mult = leaf_multipoles(new_q_ref, anterp_s, 0, anterp_s.shape[0])
        octant_parts(mult, code, child_ref, other_out_ref)


def counts_kernel(pair, octs, far_list_ref, far_op_ref, other_ref, counts_ref, rows_s):
    own, inter = far_list_ref.shape
    rows, columns = counts_ref.shape
    ops, slots, _ = rows_s.shape

    column = lax.broadcasted_iota(jnp.int32, (columns, inter), 0)
    device, slot = column // slots, column % slots
    octant = (device // 2 * 2 if pair else device - 1) * octs + slot
    op = lax.broadcasted_iota(jnp.int32, (ops, inter), 0)

    def count(g, far_list, far_op):
        source = jnp.where(octant == far_list, 1.0, 0.0).astype(BF16)
        chosen = jnp.where(op == far_op, 1.0, 0.0).astype(BF16)
        rows_s[:, pl.ds(g, 1), :] = dot_nt(chosen, source).reshape(ops, 1, columns)

    low = lax.axis_index("gz") == 0
    for g in range(own):
        count(jnp.where(low, g, octs + g) if pair else g, far_list_ref[g : g + 1], far_op_ref[g : g + 1])
    if pair:
        for g in range(octs):
            row = other_ref[g : g + 1]
            count(jnp.where(low, octs + g, g), row // ops, row % ops)
    counts_ref[...] = rows_s[...].reshape(rows, columns).astype(BF16)


def params(mib=4):
    return pltpu.CompilerParams(vmem_limit_bytes=mib << 20)


def swap(array):
    return lax.ppermute(array, "gz", [(0, 1), (1, 0)])


def beside(array, axis, width):
    count = lax.axis_size("gz")
    if count == 2:
        return swap(array)
    length = array.shape[axis]
    up = [(i, i + 1) for i in range(count - 1)]
    down = [(i + 1, i) for i in range(count - 1)]
    after = lax.ppermute(lax.slice_in_dim(array, 0, width, axis=axis), "gz", down)
    before = lax.ppermute(lax.slice_in_dim(array, length - width, length, axis=axis), "gz", up)
    return jnp.concatenate([after, before], axis)


def listed_pairs(near_list, device, pair, rows, halo):
    leaves = near_list.shape[0]
    row = jnp.arange(rows, dtype=jnp.int32)
    if pair:
        leaf = jnp.where(lax.axis_index("gz") == 0, row, leaves - 1 - row)
    else:
        leaf = jnp.where(row < leaves + halo, row, row - rows)
    leaf = leaf + device * leaves
    leaf = jnp.where(leaf < 0, -2, leaf)
    return jnp.any(near_list[:, :, None] == leaf[None, None, :], axis=1).astype(F32)


def octant_window(array):
    count = lax.axis_size("gz")
    up = [(i, i + 1) for i in range(count - 1)]
    down = [(i + 1, i) for i in range(count - 1)]
    rows = [lax.ppermute(array, "gz", up), array, lax.ppermute(array, "gz", down)]
    rows = jnp.concatenate(rows, 0)
    return jnp.pad(rows, ((0, -rows.shape[0] % 8), (0, 0)))


def shards(
    points, source, density, anterp, child_slot, child_ops, parent, near_list, far_list, far_op, translations
):
    leaves, _, width = points.shape
    octs, inter = far_list.shape
    ops, nodes, _ = translations.shape
    devices = lax.axis_size(AXES)
    pair = lax.axis_size("gz") == 2
    device = lax.axis_index(AXES)
    halo = -(-GHOST // 8) * 8

    child_row, parent_row = child_slot[None, :], parent[None, :]
    slots = -(-(2 if pair else 3) * octs // 8) * 8
    table_shape = jax.ShapeDtypeStruct((devices, slots, nodes), BF16)
    field_shape = jax.ShapeDtypeStruct((leaves, width), F32)
    table = pl.pallas_call(
        functools.partial(first_kernel, pair, octs),
        out_shape=table_shape,
        in_specs=[HBM] * 5,
        out_specs=VMEM,
        scratch_shapes=[
            pltpu.VMEM(density.shape, F32),
            pltpu.VMEM(child_row.shape, jnp.int32),
            pltpu.VMEM(parent_row.shape, jnp.int32),
            pltpu.VMEM(anterp.shape, BF16),
            pltpu.VMEM(child_ops.shape, BF16),
            pltpu.SemaphoreType.DMA((8,)),
        ],
        compiler_params=params(8),
        name="upward_pass",
    )(*map(in_hbm, (density, child_row, parent_row, anterp, child_ops)))

    points, density_sent, far_list, far_op, near_list, table = lax.optimization_barrier(
        (points, density, far_list, far_op, near_list, table)
    )
    rows = leaves + halo if pair else leaves + 2 * halo
    listed = listed_pairs(near_list, device, pair, rows, halo)
    own_points = points.transpose(1, 0, 2).reshape(3 * leaves, width)
    if pair:
        others, first_q_row = leaves, 3 * leaves
        lists = (far_list, far_op, swap(far_list * ops + far_op))
        points_other = first_q_other = swap(jnp.concatenate([own_points, density_sent], 0))
    else:
        others, first_q_row = 2 * halo, 0
        points_other = beside(own_points.reshape(3, leaves, width), 1, halo).reshape(3 * others, width)
        first_q_other = beside(density_sent, 0, halo)
        window = octant_window(far_list * ops + far_op)
        lists = (window // ops, window % ops, window)

    counts = pl.pallas_call(
        functools.partial(counts_kernel, pair, octs),
        out_shape=jax.ShapeDtypeStruct((ops * slots, devices * slots), BF16),
        in_specs=[VMEM, VMEM, VMEM],
        out_specs=VMEM,
        scratch_shapes=[pltpu.VMEM((ops, slots, devices * slots), F32)],
        compiler_params=params(4 if pair else 16),
        name="interaction_counts",
    )(*lists)

    density_now = density
    for step in range(ITERS):
        tables = lax.all_to_all(table, AXES, 0, 0, tiled=True)
        q_other, q_row = (first_q_other, (first_q_row, leaves))
        if step and pair:
            near_end = jnp.where(lax.axis_index("gz") == 0, leaves - halo, 0)
            q_other = swap(lax.dynamic_slice_in_dim(density_now, near_end, halo, axis=0))
            q_row = (0, halo)
        elif step:
            q_other = beside(density_now, 0, halo)
        near = near_start(pair, leaves, others, q_row, listed, own_points, points_other, density_now, q_other)
        last = step == ITERS - 1
        density_now, result = pl.pallas_call(
            functools.partial(later_kernel, pair, octs, last),
            out_shape=(field_shape, field_shape if last else table_shape),
            in_specs=[VMEM] * 9 + [HBM],
            out_specs=(VMEM, VMEM),
            scratch_shapes=[
                pltpu.VMEM(anterp.shape, BF16),
                pltpu.VMEM((ops, slots, nodes), F32),
                pltpu.VMEM((CHILDREN, slots, nodes), F32),
                pltpu.SemaphoreType.DMA,
            ],
            compiler_params=params(LATER_MIB),
            name="downward_upward",
        )(near, tables, counts, source, density_now, child_row, parent_row, translations, child_ops, in_hbm(anterp))
        if last:
            potential = result
        else:
            table = result
    return density_now, potential


def solution(mesh):
    rows = P(AXES, None)
    blocks = P(AXES, None, None)
    line = P(AXES)
    in_specs = (blocks, rows, rows, blocks, line, P(), line, rows, rows, rows, P())
    return jax.shard_map(shards, mesh=mesh, in_specs=in_specs, out_specs=(rows, rows), check_vma=False)
```
